32 devices in a mesh: sta: 4 (over z), grp: 2 (over y), hr: 4 (over x, core).
Axes of the slice: x: 2, y: 2, z: 4, core: 2. Of those that a mesh axis runs over, the one named last changes fastest.
Arguments:
- spectra: bfloat16 [4, 32, 6, 8192], P('hr', 'sta'), may hold values from -6 to 6
- pair_source: int32 [128], P(('sta', 'grp')), may hold values from 0 to 7
- pair_owner: int32 [128, 1], P(('sta', 'grp')), may hold values from 0 to 3; in each aligned block of 16 rows (0 to 15, 16 to 31, ...) at most 8 rows name the same one
- pair_row: int32 [128], P(('sta', 'grp')), may hold values from 0 to 7
Outputs:
- stacked: float32 [128, 9, 1024], P(('sta', 'grp'))
The draws below stay inside these ranges and needn't reach their ends.
Inputs may be any that keep to these rules, and one draw needn't show every extreme that they name: `pair_owner`: in each aligned block of 16 pairs (the pairs of one device) no value is named by more than 8 pairs, and in some block one value is named by exactly 8 pairs.
All inputs are finite; a program needn't handle non-finite values.
Results may differ from the reference program's by a relative error of at most 0.0032.
Values may be sent and summed in bfloat16 or wider, within the bound.
A program may use at most 128 MiB of HBM per device.

```python
import math
import jax
import jax.numpy as jnp
import numpy as np
from jax import lax

BINS = 8192
LAGS = 1024
STA_DEV = 8
PAIR_DEV = 16
CAP = 8
STATIONS = 32
HOURS = 4
PAIRS = 128
N_STA = 4
N_GRP = 2


def touch_ends(result, rng, least, top_value):
    spot = [jax.random.randint(jax.random.fold_in(rng, axis), (), 0, length) for axis, length in enumerate(result.shape)]
    main_axis = result.shape.index(max(result.shape))
    next_to = spot[:main_axis] + [(spot[main_axis] + 1) % result.shape[main_axis]] + spot[main_axis + 1:]
    return result.at[tuple(spot)].set(least).at[tuple(next_to)].set(top_value)


def levels(key, dims, cuts, smallest, top_value):
    def one(dim, shards_of):
        steps = jax.random.uniform(jax.random.fold_in(jax.random.fold_in(key, 6), dim), (shards_of,), jnp.float32, smallest / len(cuts), top_value / len(cuts))
        return jnp.repeat(jnp.exp(steps), dims[dim] // shards_of).reshape((-1,) + (1,) * (len(dims) - dim - 1))

    factor_of = one(*cuts[0])
    for cut in cuts[1:]:
        factor_of = factor_of * one(*cut)
    return factor_of


def shared_out(rng, own, number, rows, amount, top, bound, slope):
    order = jax.random.permutation(rng, amount)
    heavy_load, ordinary = portions_of(amount, rows * top, bound, slope, True), portions_of(amount, rows * top, bound, slope, False)
    places = jnp.arange(amount)

    def named(sizes, rotation):
        used = int((sizes > 0).sum())
        fixed = max(1, used // 4)
        moved = fixed + (places - fixed + rotation * (used - fixed)) % max(1, amount - fixed)
        return jnp.zeros((amount,), jnp.int32).at[order[jnp.where(places < fixed, places, moved)]].set(jnp.asarray(sizes, jnp.int32))

    sizes = jnp.where(number % 4 == 0, named(heavy_load, number // 4), named(ordinary, number - number // 4 - 1))
    mixed = jax.random.permutation(jax.random.fold_in(own, 3), amount)
    giver, taker = mixed[0:amount // 2 * 2:2], mixed[1:amount // 2 * 2:2]
    margin = jnp.minimum(sizes[giver] - 1, bound - sizes[taker]) // 2
    margin = jnp.where((giver == order[0]) | (taker == order[0]) | (sizes[taker] == 0), 0, jnp.maximum(margin, 0))
    moved = jax.random.randint(jax.random.fold_in(own, 4), (amount // 2,), 0, 1 << 20) % (margin + 1)
    sizes = sizes.at[giver].add(-moved).at[taker].add(moved)
    items = jnp.searchsorted(jnp.cumsum(sizes), jnp.arange(rows * top), side="right").astype(jnp.int32)
    listing = items.reshape(top, rows).T
    listing = listing[jax.random.permutation(jax.random.fold_in(own, 1), rows)]
    rotation = jax.random.randint(jax.random.fold_in(own, 2), (rows, 1), 0, top)
    return jnp.take_along_axis(listing, (jnp.arange(top)[None, :] + rotation) % top, axis=1)


def portions_of(count, total, reach, skew, full):
    portions = [(1 << 20) // math.isqrt(standing ** skew) + 1 for standing in range(1, count + 1)]
    largest = reach if full else min(reach, max(-(-total // count), total * portions[0] // sum(portions)))
    least = 1 if total - largest >= count - 1 else 0
    given, spare = [largest] + [least] * (count - 1), total - largest - least * (count - 1)
    while spare > 0:
        movable = [i for i in range(1, count) if given[i] < largest] or [i for i in range(1, count) if given[i] < reach]
        whole, left = sum([portions[i] for i in movable]), spare
        for i in movable:
            more = min(reach - given[i], max(1, left * portions[i] // whole), spare)
            given[i] = given[i] + more
            spare = spare - more
    return np.array(given)


def scatter_about(own_key, dims, width, reach, shards=(), kind=jnp.bfloat16):
    array = width * jax.random.normal(own_key, dims, jnp.float32)
    if shards:
        array = array * levels(own_key, dims, shards, -0.22, 0.18)
    return jnp.clip(array, -reach, reach).astype(kind)


def setup_inputs(seed: int = 0) -> dict:
    streams_of = jax.random.split(jax.random.key(seed), 5)
    spectra = scatter_about(streams_of[0], (HOURS, STATIONS, 6, BINS), 1.0, 6.0, ((0, 4), (1, 4)))
    pair_source = touch_ends(jax.random.randint(streams_of[1], (PAIRS,), 0, STA_DEV), jax.random.fold_in(streams_of[1], 1), 0, STA_DEV - 1).astype(jnp.int32)
    pair_owner_keys = jax.random.split(jax.random.fold_in(streams_of[2], 1), PAIRS // PAIR_DEV)
    pair_owner_turns = jax.random.permutation(jax.random.fold_in(streams_of[2], 3), PAIRS // PAIR_DEV)
    pair_owner = jax.vmap(lambda own, number: shared_out(jax.random.fold_in(streams_of[2], 2), own, number, PAIR_DEV, N_STA, 1, CAP, 2))(pair_owner_keys, pair_owner_turns).reshape((PAIRS, 1))
    pair_row = touch_ends(jax.random.randint(streams_of[3], (PAIRS,), 0, STA_DEV), jax.random.fold_in(streams_of[3], 1), 0, STA_DEV - 1).astype(jnp.int32)
    return {"spectra": spectra, "pair_source": pair_source, "pair_owner": pair_owner, "pair_row": pair_row}


two_pi = 2.0 * math.pi

def lag_table(start_bin, block_size, num_bins):
    bin_index = start_bin + jnp.arange(block_size, dtype=jnp.int32)
    lag_shift = jnp.arange(LAGS, dtype=jnp.int32) - LAGS // 2
    period = 2 * num_bins
    angles = jnp.mod(bin_index[:, None] * lag_shift[None, :], period).astype(jnp.float32) * (two_pi / period)
    return jnp.concatenate([jnp.cos(angles), -jnp.sin(angles)], axis=0).astype(jnp.bfloat16)

def cross_block(src_blk, rcv_blk):
    source_part = src_blk.astype(jnp.float32)
    recv_part = rcv_blk.astype(jnp.float32)
    src_re = source_part[..., 0:3, :][..., :, None, :]
    src_im = source_part[..., 3:6, :][..., :, None, :]
    rcv_re = recv_part[..., 0:3, :][..., None, :, :]
    rcv_im = recv_part[..., 3:6, :][..., None, :, :]
    cross_re = src_re * rcv_re + src_im * rcv_im
    cross_im = src_re * rcv_im - src_im * rcv_re
    return jnp.concatenate([cross_re, cross_im], axis=-1).astype(jnp.bfloat16)

def window_taper():
    lag_pos = jnp.arange(LAGS, dtype=jnp.float32)
    return 0.75 - 0.25 * jnp.cos(two_pi * (lag_pos + 0.5) / LAGS)

def reference(spectra, pair_source, pair_owner, pair_row):
    pair_index = jnp.arange(PAIRS, dtype=jnp.int32)
    src_station = (pair_index // (PAIR_DEV * N_GRP) * STA_DEV + pair_source).astype(jnp.int32)
    rcv_station = (pair_owner[:, 0] * STA_DEV + pair_row).astype(jnp.int32)
    group_size = math.gcd(PAIRS, 128)
    block_size = min(512, BINS)

    def one_group(ids):
        src_ids, rcv_ids = ids
        src_spec = jnp.take(spectra, src_ids, axis=1)
        rcv_spec = jnp.take(spectra, rcv_ids, axis=1)

        def add_block(block_index, running):
            start_bin = (block_index * block_size).astype(jnp.int32)
            src_blk = lax.dynamic_slice_in_dim(src_spec, start_bin, block_size, 3)
            rcv_blk = lax.dynamic_slice_in_dim(rcv_spec, start_bin, block_size, 3)
            cross = lax.optimization_barrier(cross_block(src_blk, rcv_blk))
            summed = lax.optimization_barrier(jnp.sum(cross.astype(jnp.float32), axis=0)).reshape(group_size * 9, 2 * block_size)
            table = lax.optimization_barrier(lag_table(start_bin, block_size, BINS)).astype(jnp.float32)
            return running + jnp.dot(summed, table, precision=lax.Precision.HIGHEST)
        running = lax.fori_loop(0, BINS // block_size, add_block, jnp.zeros((group_size * 9, LAGS), jnp.float32))
        return running.reshape(group_size, 9, LAGS)
    corr = lax.map(one_group, (src_station.reshape(-1, group_size), rcv_station.reshape(-1, group_size)))
    corr = corr.reshape(PAIRS, 9, LAGS)
    return corr * window_taper()[None, None, :] / (HOURS * math.sqrt(BINS))
```

```python
import functools
import math

import jax
import jax.numpy as jnp
import numpy as np
from jax import lax
from jax.experimental import pallas as pl
from jax.experimental.pallas import tpu as pltpu
from jax.sharding import PartitionSpec as P

LAGS = 1024
STEP = 64
two_pi = 2.0 * math.pi
MESH = pl.DeviceIdType.MESH


def angle_tables(num_bins):
    period = 2 * num_bins
    shift = np.arange(LAGS) - LAGS // 2

    def pair(bins):
        angles = np.mod(bins[:, None] * shift[None, :], period) * (two_pi / period)
        return np.cos(angles).astype(np.float32), np.sin(angles).astype(np.float32)

    return pair(np.arange(0, num_bins, STEP)) + pair(np.arange(STEP))


def window_taper():
    lag_pos = np.arange(LAGS, dtype=np.float64)
    return 0.75 - 0.25 * np.cos(two_pi * (lag_pos + 0.5) / LAGS)


def kernel(
    n, groups, hours, pairs, chunk, chunks,
    spec_ref, pick_ref, coarse_cos, coarse_sin, fine_cos, fine_sin, taper_ref,
    out_ref,
    gathered, picks, table, src, rcv, cross, acc, partial, landed, final,
    send_sem, recv_sem, pick_send, pick_recv, part_send, part_recv, fin_send, fin_recv,
):
    z = lax.axis_index("sta")
    g = lax.axis_index("grp")
    h = lax.axis_index("hr")
    plane = groups * hours
    me = g * hours + h
    block = spec_ref.shape[0]
    pick_rows = pick_ref.shape[0]
    rows = 9 * pairs
    part = LAGS // hours

    barrier = pltpu.get_barrier_semaphore()

    @pl.loop(1, plane)
    def _(d):
        t = lax.rem(me + d, plane)
        pl.semaphore_signal(
            barrier, inc=1, device_id={"grp": t // hours, "hr": lax.rem(t, hours)}, device_id_type=MESH
        )

    @pl.when(z > 0)
    def _():
        pl.semaphore_signal(barrier, inc=1, device_id={"sta": z - 1}, device_id_type=MESH)

    @pl.when(z < n - 1)
    def _():
        pl.semaphore_signal(barrier, inc=1, device_id={"sta": z + 1}, device_id_type=MESH)

    pl.semaphore_wait(barrier, plane - 1 + (z > 0).astype(jnp.int32) + (z < n - 1).astype(jnp.int32))

    def at_chunk(ref, b, c):
        return ref.at[pl.ds(pl.multiple_of(b * block, 16), block), pl.ds(pl.multiple_of(c * chunk, 128), chunk)]

    def line_copy(b, c, side, own):
        return pltpu.make_async_remote_copy(
            src_ref=at_chunk(spec_ref, 0, c) if own else at_chunk(gathered, b, c),
            dst_ref=at_chunk(gathered, b, c),
            send_sem=send_sem.at[side, b, c],
            recv_sem=recv_sem.at[b, c],
            device_id={"sta": z + 1 if side == 0 else z - 1},
            device_id_type=MESH,
        )

    @pl.loop(0, chunks)
    def _(c):
        @pl.when(z < n - 1)
        def _():
            line_copy(z, c, 0, True).start()

        @pl.when(z > 0)
        def _():
            line_copy(z, c, 1, True).start()

    def pick_copy(d):
        return pltpu.make_async_remote_copy(
            src_ref=pick_ref,
            dst_ref=picks.at[g],
            send_sem=pick_send.at[d],
            recv_sem=pick_recv.at[d],
            device_id={"grp": lax.rem(g + d, groups)},
            device_id_type=MESH,
        )

    @pl.loop(1, groups)
    def _(d):
        pick_copy(d).start()

    picks[g] = pick_ref[...]
    gathered[pl.ds(pl.multiple_of(z * block, 16), block), :] = spec_ref[...]
    acc[...] = jnp.zeros_like(acc)

    def arrive(k, c):
        @pl.when(z - k >= 0)
        def _():
            line_copy(z - k, c, 0, False).wait_recv()

            @pl.when(z < n - 1)
            def _():
                line_copy(z - k, c, 0, False).start()

        @pl.when(z + k < n)
        def _():
            line_copy(z + k, c, 1, False).wait_recv()

            @pl.when(z > 0)
            def _():
                line_copy(z + k, c, 1, False).start()

    steps = chunk // STEP

    def make_table(c):
        @pl.loop(0, steps)
        def _(i):
            row = g * (chunks * steps) + c * steps + i
            ca = coarse_cos[pl.ds(row, 1), :]
            sa = coarse_sin[pl.ds(row, 1), :]
            at = pl.multiple_of(c * (2 * chunk) + i * STEP, STEP)
            for r in range(0, STEP, 16):
                cb = fine_cos[r:r + 16, :]
                sb = fine_sin[r:r + 16, :]
                table[pl.ds(at + r, 16), :] = (ca * cb - sa * sb).astype(jnp.bfloat16)
                table[pl.ds(at + chunk + r, 16), :] = -(sa * cb + ca * sb).astype(jnp.bfloat16)

    def compute(c):
        here = pl.ds(pl.multiple_of(c * chunk, 128), chunk)
        own = spec_ref[:, here]
        every = gathered[:, here]
        for q in range(groups):
            src[q * pick_rows:(q + 1) * pick_rows, :] = jnp.dot(
                picks[q, :, n * block:(n + 1) * block], own, preferred_element_type=jnp.float32
            )
            rcv[q * pick_rows:(q + 1) * pick_rows, :] = jnp.dot(
                picks[q, :, 0:n * block], every, preferred_element_type=jnp.float32
            )

        @pl.loop(0, groups)
        def _(q):
            base = pl.multiple_of(q * pick_rows, 16)
            top = pl.multiple_of(q * rows, 16)
            for lane in range(0, chunk, 128):
                s = [src[pl.ds(base + pairs * k, pairs), lane:lane + 128] for k in range(6)]
                r = [rcv[pl.ds(base + pairs * k, pairs), lane:lane + 128] for k in range(6)]
                for a in range(3):
                    for b in range(3):
                        spot = pl.ds(top + (3 * a + b) * pairs, pairs)
                        cross[spot, lane:lane + 128] = (s[a] * r[b] + s[3 + a] * r[3 + b]).astype(jnp.bfloat16)
                        cross[spot, chunk + lane:chunk + lane + 128] = (
                            s[a] * r[3 + b] - s[3 + a] * r[b]
                        ).astype(jnp.bfloat16)

        acc[...] += jnp.dot(
            cross[...],
            table[pl.ds(pl.multiple_of(c * (2 * chunk), 16), 2 * chunk), :],
            preferred_element_type=jnp.float32,
        )

    @pl.loop(0, chunks)
    def _(c):
        make_table(c)
        arrive(1, c)

    @pl.loop(2, n - 1)
    def _(k):
        @pl.loop(0, chunks)
        def _(c):
            arrive(k, c)

    @pl.loop(1, groups)
    def _(d):
        pick_copy(d).wait()

    @pl.loop(0, chunks)
    def _(c):
        if n > 2:
            arrive(n - 1, c)
        compute(c)

    partial[...] = acc[...].astype(jnp.bfloat16)

    def part_copy(d):
        t = lax.rem(me + d, plane)
        tg, th = t // hours, lax.rem(t, hours)
        return pltpu.make_async_remote_copy(
            src_ref=partial.at[pl.ds(pl.multiple_of(tg * rows, 16), rows), pl.ds(pl.multiple_of(th * part, 128), part)],
            dst_ref=landed.at[d],
            send_sem=part_send.at[d],
            recv_sem=part_recv.at[d],
            device_id={"grp": tg, "hr": th},
            device_id_type=MESH,
        )

    @pl.loop(1, plane)
    def _(d):
        part_copy(d).start()

    lags = pl.ds(pl.multiple_of(h * part, 128), part)
    final[...] = acc[pl.ds(pl.multiple_of(g * rows, 16), rows), lags]

    @pl.loop(1, plane)
    def _(d):
        part_copy(d).wait_recv()
        final[...] += landed[d].astype(jnp.float32)

    out_ref[:, lags] = (final[...] * taper_ref[:, lags]).astype(jnp.bfloat16)

    def fin_copy(d):
        return pltpu.make_async_remote_copy(
            src_ref=out_ref.at[:, lags],
            dst_ref=out_ref.at[:, lags],
            send_sem=fin_send.at[d],
            recv_sem=fin_recv.at[d],
            device_id={"hr": lax.rem(h + d, hours)},
            device_id_type=MESH,
        )

    @pl.loop(1, hours)
    def _(d):
        fin_copy(d).start()

    @pl.loop(1, plane)
    def _(d):
        part_copy(d).wait_send()

    @pl.loop(0, n - 1)
    def _(k):
        @pl.loop(0, chunks)
        def _(c):
            @pl.when((z - k >= 0) & (z < n - 1))
            def _():
                line_copy(z - k, c, 0, True).wait_send()

            @pl.when((z + k < n) & (z > 0))
            def _():
                line_copy(z + k, c, 1, True).wait_send()

    @pl.loop(1, hours)
    def _(d):
        fin_copy(d).wait()


def body(n, groups, hours, spectra, pair_source, pair_owner, pair_row):
    _, sta_dev, comps, num_bins = spectra.shape
    pairs = pair_source.shape[0]
    bins = num_bins // groups
    chunk = min(512, bins)
    chunks = bins // chunk
    block = comps * sta_dev
    pick_rows = comps * pairs
    width = -(-((n + 1) * block) // 128) * 128

    start = lax.axis_index("grp") * bins
    mine = lax.dynamic_slice_in_dim(spectra[0], start, bins, 2)
    spec = jnp.transpose(mine, (1, 0, 2)).reshape(block, bins)

    comp_at = (jnp.arange(comps, dtype=jnp.int32) * sta_dev)[:, None]
    wanted = (comp_at + (pair_owner[:, 0] * block + pair_row)[None, :]).reshape(pick_rows, 1)
    origin = (comp_at + (n * block + pair_source)[None, :]).reshape(pick_rows, 1)
    column = jnp.arange(width, dtype=jnp.int32)[None, :]
    pick = ((wanted == column) | (origin == column)).astype(jnp.bfloat16)

    taper = (window_taper() / (hours * spectra.shape[0] * math.sqrt(num_bins))).astype(np.float32)[None, :]
    tables = angle_tables(num_bins)
    rows = 9 * pairs
    plane = groups * hours
    vmem = pl.BlockSpec(memory_space=pltpu.VMEM)
    out = pl.pallas_call(
        functools.partial(kernel, n, groups, hours, pairs, chunk, chunks),
        out_shape=jax.ShapeDtypeStruct((rows, LAGS), jnp.bfloat16),
        in_specs=[vmem] * 7,
        out_specs=vmem,
        scratch_shapes=[
            pltpu.VMEM((n * block, bins), jnp.bfloat16),
            pltpu.VMEM((groups, pick_rows, width), jnp.bfloat16),
            pltpu.VMEM((2 * bins, LAGS), jnp.bfloat16),
            pltpu.VMEM((groups * pick_rows, chunk), jnp.float32),
            pltpu.VMEM((groups * pick_rows, chunk), jnp.float32),
            pltpu.VMEM((groups * rows, 2 * chunk), jnp.bfloat16),
            pltpu.VMEM((groups * rows, LAGS), jnp.float32),
            pltpu.VMEM((groups * rows, LAGS), jnp.bfloat16),
            pltpu.VMEM((plane, rows, LAGS // hours), jnp.bfloat16),
            pltpu.VMEM((rows, LAGS // hours), jnp.float32),
            pltpu.SemaphoreType.DMA((2, n, chunks)),
            pltpu.SemaphoreType.DMA((n, chunks)),
            pltpu.SemaphoreType.DMA((groups,)),
            pltpu.SemaphoreType.DMA((groups,)),
            pltpu.SemaphoreType.DMA((plane,)),
            pltpu.SemaphoreType.DMA((plane,)),
            pltpu.SemaphoreType.DMA((hours,)),
            pltpu.SemaphoreType.DMA((hours,)),
        ],
        compiler_params=pltpu.CompilerParams(
            collective_id=0, has_side_effects=True, vmem_limit_bytes=48 * 1024 * 1024
        ),
        cost_estimate=pl.CostEstimate(
            flops=4 * groups * rows * bins * LAGS, bytes_accessed=4 * block * bins, transcendentals=0
        ),
    )(spec, pick, *[jnp.asarray(t) for t in tables], jnp.asarray(taper))
    return jnp.transpose(out.reshape(9, pairs, LAGS), (1, 0, 2)).astype(jnp.float32)


def solution(mesh):
    placed = (
        P("hr", "sta", None, None),
        P(("sta", "grp")),
        P(("sta", "grp"), None),
        P(("sta", "grp")),
    )
    sizes = (mesh.shape["sta"], mesh.shape["grp"], mesh.shape["hr"])
    return jax.shard_map(
        functools.partial(body, *sizes),
        mesh=mesh,
        in_specs=placed,
        out_specs=P(("sta", "grp"), None, None),
        check_vma=False,
    )
```

```python
import functools
import math

import jax
import jax.numpy as jnp
import numpy as np
from jax import lax
from jax.experimental import pallas as pl
from jax.experimental.pallas import tpu as pltpu
from jax.sharding import PartitionSpec as P

LAGS = 1024
STEP = 64
two_pi = 2.0 * math.pi
MESH = pl.DeviceIdType.MESH


def angle_tables(num_bins):
    period = 2 * num_bins
    shift = np.arange(LAGS) - LAGS // 2

    def pair(bins):
        angles = np.mod(bins[:, None] * shift[None, :], period) * (two_pi / period)
        return np.cos(angles).astype(np.float32), np.sin(angles).astype(np.float32)

    return pair(np.arange(0, num_bins, STEP)) + pair(np.arange(STEP))


def window_taper():
    lag_pos = np.arange(LAGS, dtype=np.float64)
    return 0.75 - 0.25 * np.cos(two_pi * (lag_pos + 0.5) / LAGS)


def kernel(
    n, groups, hours, pairs, chunk, chunks, helped, ahead,
    spec_ref, pick_ref, tables_ref, taper_ref,
    out_ref,
    gathered, picks, coarse_cos, coarse_sin, fine_cos, fine_sin, table, src, rcv, cross, acc, partial, landed, final,
    handed,
    send_sem, recv_sem, pick_send, pick_recv, give_send, give_recv, part_send, part_recv, fin_send, fin_recv,
    hand_send, hand_recv, table_sem,
):
    z = lax.axis_index("sta")
    g = lax.axis_index("grp")
    h = lax.axis_index("hr")
    plane = groups * hours
    me = g * hours + h
    block = spec_ref.shape[0]
    pick_rows = pick_ref.shape[0]
    rows = 9 * pairs
    part = LAGS // hours
    steps = chunk // STEP
    edge = (z == 0) | (z == n - 1)
    helper = (z == 1) | (z == n - 2)
    partner = jnp.where(z == 0, 1, jnp.where(z == 1, 0, jnp.where(z == n - 1, n - 2, n - 1)))

    def table_copy(i):
        if i < 2:
            rows_here = chunks * steps
            first = i * (groups * rows_here) + g * rows_here
            return pltpu.make_async_copy(
                tables_ref.at[pl.ds(pl.multiple_of(first, 8), rows_here)],
                (coarse_cos, coarse_sin)[i], table_sem.at[i],
            )
        first = 2 * groups * chunks * steps + (i - 2) * STEP
        return pltpu.make_async_copy(
            tables_ref.at[pl.ds(first, STEP)], (fine_cos, fine_sin)[i - 2], table_sem.at[i]
        )

    for i in range(4):
        table_copy(i).start()

    barrier = pltpu.get_barrier_semaphore()

    @pl.loop(1, plane)
    def _(d):
        t = lax.rem(me + d, plane)
        pl.semaphore_signal(
            barrier, inc=1, device_id={"grp": t // hours, "hr": lax.rem(t, hours)}, device_id_type=MESH
        )

    @pl.when(z > 0)
    def _():
        pl.semaphore_signal(barrier, inc=1, device_id={"sta": z - 1}, device_id_type=MESH)

    @pl.when(z < n - 1)
    def _():
        pl.semaphore_signal(barrier, inc=1, device_id={"sta": z + 1}, device_id_type=MESH)

    expected = plane - 1 + (z > 0).astype(jnp.int32) + (z < n - 1).astype(jnp.int32)
    if helped:
        @pl.when(edge | helper)
        def _():
            @pl.loop(1, groups)
            def _(d):
                pl.semaphore_signal(
                    barrier, inc=1, device_id={"sta": partner, "grp": lax.rem(g + d, groups)}, device_id_type=MESH
                )

        expected = expected + (groups - 1) * (edge | helper).astype(jnp.int32)
    pl.semaphore_wait(barrier, expected)

    def at_chunk(ref, b, c):
        return ref.at[pl.ds(pl.multiple_of(b * block, 16), block), pl.ds(pl.multiple_of(c * chunk, 128), chunk)]

    def line_copy(b, c, side, own):
        return pltpu.make_async_remote_copy(
            src_ref=at_chunk(spec_ref, 0, c) if own else at_chunk(gathered, b, c),
            dst_ref=at_chunk(gathered, b, c),
            send_sem=send_sem.at[side, b, c],
            recv_sem=recv_sem.at[b, c],
            device_id={"sta": z + 1 if side == 0 else z - 1},
            device_id_type=MESH,
        )

    def goes_right(c):
        return (z < n - 2) | ((z == n - 2) & (c >= helped))

    def goes_left(c):
        return (z > 1) | ((z == 1) & (c >= helped))

    def send_own(c):
        @pl.when(goes_right(c))
        def _():
            line_copy(z, c, 0, True).start()

        @pl.when(goes_left(c))
        def _():
            line_copy(z, c, 1, True).start()

    def pick_copy(d):
        return pltpu.make_async_remote_copy(
            src_ref=pick_ref,
            dst_ref=picks.at[0, pl.ds(pl.multiple_of(g * pick_rows, 16), pick_rows)],
            send_sem=pick_send.at[d],
            recv_sem=pick_recv.at[d],
            device_id={"grp": lax.rem(g + d, groups)},
            device_id_type=MESH,
        )

    def give_copy(d):
        return pltpu.make_async_remote_copy(
            src_ref=pick_ref,
            dst_ref=picks.at[1, pl.ds(pl.multiple_of(g * pick_rows, 16), pick_rows)],
            send_sem=give_send.at[d],
            recv_sem=give_recv.at[d],
            device_id={"sta": partner, "grp": lax.rem(g + d, groups)},
            device_id_type=MESH,
        )

    @pl.loop(0, min(ahead, chunks))
    def _(c):
        send_own(c)

    @pl.loop(1, groups)
    def _(d):
        pick_copy(d).start()

    if helped:
        @pl.when(edge)
        def _():
            @pl.loop(0, groups)
            def _(d):
                give_copy(d).start()

    picks[0, pl.ds(pl.multiple_of(g * pick_rows, 16), pick_rows), :] = pick_ref[...]
    gathered[pl.ds(pl.multiple_of(z * block, 16), block), :] = spec_ref[...]
    acc[...] = jnp.zeros_like(acc)

    def arrive(k, c):
        wanted = (c >= helped) | jnp.logical_not(edge)

        @pl.when((z - k >= 0) & wanted)
        def _():
            line_copy(z - k, c, 0, False).wait_recv()

            @pl.when(goes_right(c))
            def _():
                line_copy(z - k, c, 0, False).start()

        @pl.when((z + k < n) & wanted)
        def _():
            line_copy(z + k, c, 1, False).wait_recv()

            @pl.when(goes_left(c))
            def _():
                line_copy(z + k, c, 1, False).start()

    def make_table(c):
        @pl.loop(0, steps)
        def _(i):
            row = c * steps + i
            ca = coarse_cos[pl.ds(row, 1), :]
            sa = coarse_sin[pl.ds(row, 1), :]
            at = pl.multiple_of(c * (2 * chunk) + i * STEP, STEP)
            for r in range(0, STEP, 16):
                cb = fine_cos[r:r + 16, :]
                sb = fine_sin[r:r + 16, :]
                table[pl.ds(at + r, 16), :] = (ca * cb - sa * sb).astype(jnp.bfloat16)
                table[pl.ds(at + chunk + r, 16), :] = -(sa * cb + ca * sb).astype(jnp.bfloat16)

    def compute(w, c):
        here = pl.ds(pl.multiple_of(c * chunk, 128), chunk)
        origin = jnp.where(w == 0, z, partner)
        own = gathered[pl.ds(pl.multiple_of(origin * block, 16), block), here]
        src[...] = jnp.dot(
            picks[w, :, n * block:(n + 1) * block], own, preferred_element_type=jnp.float32
        )
        rcv[...] = jnp.dot(
            picks[w, :, 0:n * block], gathered[:, here], preferred_element_type=jnp.float32
        )

        @pl.loop(0, groups)
        def _(q):
            base = pl.multiple_of(q * pick_rows, 16)
            top = pl.multiple_of(q * rows, 16)
            for lane in range(0, chunk, 128):
                s = [src[pl.ds(base + pairs * k, pairs), lane:lane + 128] for k in range(6)]
                r = [rcv[pl.ds(base + pairs * k, pairs), lane:lane + 128] for k in range(6)]
                for a in range(3):
                    for b in range(3):
                        spot = pl.ds(top + (3 * a + b) * pairs, pairs)
                        cross[spot, lane:lane + 128] = (s[a] * r[b] + s[3 + a] * r[3 + b]).astype(jnp.bfloat16)
                        cross[spot, chunk + lane:chunk + lane + 128] = (
                            s[a] * r[3 + b] - s[3 + a] * r[b]
                        ).astype(jnp.bfloat16)

        acc[w] += jnp.dot(
            cross[...],
            table[pl.ds(pl.multiple_of(c * (2 * chunk), 16), 2 * chunk), :],
            preferred_element_type=jnp.float32,
        )

    lags = pl.ds(pl.multiple_of(h * part, 128), part)
    own_rows = pl.ds(pl.multiple_of(g * rows, 16), rows)

    def part_copy(w, d):
        t = lax.rem(me + d, plane)
        tg, th = t // hours, lax.rem(t, hours)
        return pltpu.make_async_remote_copy(
            src_ref=partial.at[
                w, pl.ds(pl.multiple_of(tg * rows, 16), rows), pl.ds(pl.multiple_of(th * part, 128), part)
            ],
            dst_ref=landed.at[w, d],
            send_sem=part_send.at[w, d],
            recv_sem=part_recv.at[w, d],
            device_id={"grp": tg, "hr": th},
            device_id_type=MESH,
        )

    def scatter(w):
        partial[w] = acc[w].astype(jnp.bfloat16)

        @pl.loop(1, plane)
        def _(d):
            part_copy(w, d).start()

    def collect(w):
        final[...] = acc[w, own_rows, lags]

        @pl.loop(1, plane)
        def _(d):
            part_copy(w, d).wait_recv()
            final[...] += landed[w, d].astype(jnp.float32)

    def hand_copy():
        return pltpu.make_async_remote_copy(
            src_ref=handed,
            dst_ref=landed.at[0, 0],
            send_sem=hand_send,
            recv_sem=hand_recv,
            device_id={"sta": partner},
            device_id_type=MESH,
        )

    for i in range(4):
        table_copy(i).wait()

    lag_steps = max(n - 2, 0)

    @pl.loop(0, chunks + lag_steps)
    def _(it):
        @pl.when(it + ahead < chunks)
        def _():
            send_own(it + ahead)

        @pl.when((it < chunks) & ((it >= helped) | jnp.logical_not(edge)))
        def _():
            make_table(it)

        @pl.loop(1, n)
        def _(k):
            c = it - (k - 1)

            @pl.when((c >= 0) & (c < chunks))
            def _():
                arrive(k, c)

        @pl.when(it == lag_steps)
        def _():
            @pl.loop(1, groups)
            def _(d):
                pick_copy(d).wait()

            if helped:
                @pl.when(helper)
                def _():
                    @pl.loop(0, groups)
                    def _(d):
                        give_copy(d).wait_recv()

        c = it - lag_steps
        turns = jnp.where(c >= helped, 1, jnp.where(edge, 0, jnp.where(helper, 2, 1)))

        @pl.loop(0, jnp.where(c >= 0, turns, 0))
        def _(w):
            compute(w, c)

        if helped:
            @pl.when(helper & (c == helped - 1))
            def _():
                scatter(1)

            @pl.when(helper & (c == helped + 1))
            def _():
                collect(1)
                handed[...] = final[...].astype(jnp.bfloat16)
                hand_copy().start()

    scatter(0)
    collect(0)
    if helped:
        @pl.when(edge)
        def _():
            hand_copy().wait_recv()
            final[...] += landed[0, 0].astype(jnp.float32)

    out_ref[:, lags] = (final[...] * taper_ref[:, lags]).astype(jnp.bfloat16)

    def fin_copy(d):
        return pltpu.make_async_remote_copy(
            src_ref=out_ref.at[:, lags],
            dst_ref=out_ref.at[:, lags],
            send_sem=fin_send.at[d],
            recv_sem=fin_recv.at[d],
            device_id={"hr": lax.rem(h + d, hours)},
            device_id_type=MESH,
        )

    @pl.loop(1, hours)
    def _(d):
        fin_copy(d).start()

    @pl.loop(1, plane)
    def _(d):
        part_copy(0, d).wait_send()

    if helped:
        @pl.when(helper)
        def _():
            hand_copy().wait_send()

            @pl.loop(1, plane)
            def _(d):
                part_copy(1, d).wait_send()

        @pl.when(edge)
        def _():
            @pl.loop(0, groups)
            def _(d):
                give_copy(d).wait_send()

    @pl.loop(0, n - 1)
    def _(k):
        @pl.loop(0, chunks)
        def _(c):
            @pl.when((z - k >= 0) & goes_right(c))
            def _():
                line_copy(z - k, c, 0, True).wait_send()

            @pl.when((z + k < n) & goes_left(c))
            def _():
                line_copy(z + k, c, 1, True).wait_send()

    @pl.loop(1, hours)
    def _(d):
        fin_copy(d).wait()


def body(n, groups, hours, spectra, pair_source, pair_owner, pair_row):
    _, sta_dev, comps, num_bins = spectra.shape
    pairs = pair_source.shape[0]
    bins = num_bins // groups
    chunk = min(512, bins)
    chunks = bins // chunk
    helped = 3 * chunks // 8 if n >= 4 else 0
    held = 2 if helped else 1
    block = comps * sta_dev
    pick_rows = comps * pairs
    width = -(-((n + 1) * block) // 128) * 128

    start = lax.axis_index("grp") * bins
    mine = lax.dynamic_slice_in_dim(spectra[0], start, bins, 2)
    spec = jnp.transpose(mine, (1, 0, 2)).reshape(block, bins)

    comp_at = (jnp.arange(comps, dtype=jnp.int32) * sta_dev)[:, None]
    wanted = (comp_at + (pair_owner[:, 0] * block + pair_row)[None, :]).reshape(pick_rows, 1)
    origin = (comp_at + (n * block + pair_source)[None, :]).reshape(pick_rows, 1)
    column = jnp.arange(width, dtype=jnp.int32)[None, :]
    pick = ((wanted == column) | (origin == column)).astype(jnp.bfloat16)

    taper = (window_taper() / (hours * spectra.shape[0] * math.sqrt(num_bins))).astype(np.float32)[None, :]
    tables = angle_tables(num_bins)
    rows = 9 * pairs
    plane = groups * hours
    vmem = pl.BlockSpec(memory_space=pltpu.VMEM)
    hbm = pl.BlockSpec(memory_space=pltpu.HBM)
    coarse = pltpu.VMEM((bins // STEP, LAGS), jnp.float32)
    fine = pltpu.VMEM((STEP, LAGS), jnp.float32)
    out = pl.pallas_call(
        functools.partial(kernel, n, groups, hours, pairs, chunk, chunks, helped, 3),
        out_shape=jax.ShapeDtypeStruct((rows, LAGS), jnp.bfloat16),
        in_specs=[vmem, vmem, hbm, vmem],
        out_specs=vmem,
        scratch_shapes=[
            pltpu.VMEM((n * block, bins), jnp.bfloat16),
            pltpu.VMEM((held, groups * pick_rows, width), jnp.bfloat16),
            coarse, coarse, fine, fine,
            pltpu.VMEM((2 * bins, LAGS), jnp.bfloat16),
            pltpu.VMEM((groups * pick_rows, chunk), jnp.float32),
            pltpu.VMEM((groups * pick_rows, chunk), jnp.float32),
            pltpu.VMEM((groups * rows, 2 * chunk), jnp.bfloat16),
            pltpu.VMEM((held, groups * rows, LAGS), jnp.float32),
            pltpu.VMEM((held, groups * rows, LAGS), jnp.bfloat16),
            pltpu.VMEM((held, plane, rows, LAGS // hours), jnp.bfloat16),
            pltpu.VMEM((rows, LAGS // hours), jnp.float32),
            pltpu.VMEM((rows, LAGS // hours), jnp.bfloat16),
            pltpu.SemaphoreType.DMA((2, n, chunks)),
            pltpu.SemaphoreType.DMA((n, chunks)),
            pltpu.SemaphoreType.DMA((groups,)),
            pltpu.SemaphoreType.DMA((groups,)),
            pltpu.SemaphoreType.DMA((groups,)),
            pltpu.SemaphoreType.DMA((groups,)),
            pltpu.SemaphoreType.DMA((held, plane)),
            pltpu.SemaphoreType.DMA((held, plane)),
            pltpu.SemaphoreType.DMA((hours,)),
            pltpu.SemaphoreType.DMA((hours,)),
            pltpu.SemaphoreType.DMA,
            pltpu.SemaphoreType.DMA,
            pltpu.SemaphoreType.DMA((4,)),
        ],
        compiler_params=pltpu.CompilerParams(
            collective_id=0, has_side_effects=True, vmem_limit_bytes=48 * 1024 * 1024
        ),
        cost_estimate=pl.CostEstimate(
            flops=4 * groups * rows * bins * LAGS, bytes_accessed=4 * block * bins, transcendentals=0
        ),
    )(spec, pick, jnp.asarray(np.concatenate(tables)), jnp.asarray(taper))
    return jnp.transpose(out.reshape(9, pairs, LAGS), (1, 0, 2)).astype(jnp.float32)


def solution(mesh):
    placed = (
        P("hr", "sta", None, None),
        P(("sta", "grp")),
        P(("sta", "grp"), None),
        P(("sta", "grp")),
    )
    sizes = (mesh.shape["sta"], mesh.shape["grp"], mesh.shape["hr"])
    return jax.shard_map(
        functools.partial(body, *sizes),
        mesh=mesh,
        in_specs=placed,
        out_specs=P(("sta", "grp"), None, None),
        check_vma=False,
    )
```

```python
import functools
import math

import jax
import jax.numpy as jnp
from jax import lax
from jax.experimental import pallas as pl
from jax.experimental.pallas import tpu as pltpu
from jax.sharding import PartitionSpec as P

LAGS = 1024
STEP = 64
two_pi = 2.0 * math.pi
MESH = pl.DeviceIdType.MESH


def turn(first, step, num_bins):
    period = 2 * num_bins
    bins = first + step * lax.broadcasted_iota(jnp.int32, (8, LAGS), 0)
    shift = lax.broadcasted_iota(jnp.int32, (8, LAGS), 1) - LAGS // 2
    angle = (((bins * shift + num_bins) & (period - 1)) - num_bins).astype(jnp.float32) * (two_pi / period)
    return jnp.cos(angle), jnp.sin(angle)


def kernel(
    n, groups, hours, pairs, chunk, chunks, helped, ahead, slack, scale,
    spec_ref, pick_ref,
    out_ref,
    gathered, picks, coarse_cos, coarse_sin, fine_cos, fine_sin, table, src, rcv, cross, acc, partial, landed, final,
    handed,
    send_sem, recv_sem, pick_send, pick_recv, give_send, give_recv, part_send, part_recv, fin_send, fin_recv,
    hand_send, hand_recv,
):
    z = lax.axis_index("sta")
    g = lax.axis_index("grp")
    h = lax.axis_index("hr")
    plane = groups * hours
    me = g * hours + h
    block = spec_ref.shape[0]
    pick_rows = pick_ref.shape[0]
    rows = 9 * pairs
    part = LAGS // hours
    steps = chunk // STEP
    edge = (z == 0) | (z == n - 1)
    helper = (z == 1) | (z == n - 2)
    partner = jnp.where(z == 0, 1, jnp.where(z == 1, 0, jnp.where(z == n - 1, n - 2, n - 1)))

    for c in range(chunks):
        gathered[c, pl.ds(pl.multiple_of(z * block, 16), block), :] = spec_ref[:, c * chunk:(c + 1) * chunk]

    barrier = pltpu.get_barrier_semaphore()

    @pl.loop(1, plane)
    def _(d):
        t = lax.rem(me + d, plane)
        pl.semaphore_signal(
            barrier, inc=1, device_id={"grp": t // hours, "hr": lax.rem(t, hours)}, device_id_type=MESH
        )

    @pl.when(z > 0)
    def _():
        pl.semaphore_signal(barrier, inc=1, device_id={"sta": z - 1}, device_id_type=MESH)

    @pl.when(z < n - 1)
    def _():
        pl.semaphore_signal(barrier, inc=1, device_id={"sta": z + 1}, device_id_type=MESH)

    expected = plane - 1 + (z > 0).astype(jnp.int32) + (z < n - 1).astype(jnp.int32)
    if helped:
        @pl.when(edge | helper)
        def _():
            @pl.loop(1, groups)
            def _(d):
                pl.semaphore_signal(
                    barrier, inc=1, device_id={"sta": partner, "grp": lax.rem(g + d, groups)}, device_id_type=MESH
                )

        expected = expected + (groups - 1) * (edge | helper).astype(jnp.int32)
    pl.semaphore_wait(barrier, expected)

    def line_copy(b, c, side):
        spot = gathered.at[c, pl.ds(pl.multiple_of(b * block, 16), block)]
        return pltpu.make_async_remote_copy(
            src_ref=spot,
            dst_ref=spot,
            send_sem=send_sem.at[side, b, c],
            recv_sem=recv_sem.at[b, c],
            device_id={"sta": z + 1 if side == 0 else z - 1},
            device_id_type=MESH,
        )

    def goes_right(c):
        return (z < n - 2) | ((z == n - 2) & (c >= helped))

    def goes_left(c):
        return (z > 1) | ((z == 1) & (c >= helped))

    def send_own(c):
        @pl.when(goes_right(c))
        def _():
            line_copy(z, c, 0).start()

        @pl.when(goes_left(c))
        def _():
            line_copy(z, c, 1).start()

    def pick_copy(d):
        return pltpu.make_async_remote_copy(
            src_ref=pick_ref,
            dst_ref=picks.at[0, pl.ds(pl.multiple_of(g * pick_rows, 16), pick_rows)],
            send_sem=pick_send.at[d],
            recv_sem=pick_recv.at[d],
            device_id={"grp": lax.rem(g + d, groups)},
            device_id_type=MESH,
        )

    def give_copy(d):
        return pltpu.make_async_remote_copy(
            src_ref=pick_ref,
            dst_ref=picks.at[1, pl.ds(pl.multiple_of(g * pick_rows, 16), pick_rows)],
            send_sem=give_send.at[d],
            recv_sem=give_recv.at[d],
            device_id={"sta": partner, "grp": lax.rem(g + d, groups)},
            device_id_type=MESH,
        )

    @pl.loop(0, min(ahead, chunks))
    def _(c):
        send_own(c)

    @pl.loop(1, groups)
    def _(d):
        pick_copy(d).start()

    if helped:
        @pl.when(edge)
        def _():
            @pl.loop(0, groups)
            def _(d):
                give_copy(d).start()

    picks[0, pl.ds(pl.multiple_of(g * pick_rows, 16), pick_rows), :] = pick_ref[...]
    acc[...] = jnp.zeros_like(acc)

    num_bins = groups * chunks * chunk

    def outer(cos_ref, sin_ref, count, first, step):
        lc, ls = turn(0, step, num_bins)
        hc, hs = turn(first, 8 * step, num_bins)
        for i in range(count // 8):
            a, b = hc[i:i + 1, :], hs[i:i + 1, :]
            cos_ref[8 * i:8 * i + 8, :] = a * lc - b * ls
            sin_ref[8 * i:8 * i + 8, :] = b * lc + a * ls

    outer(fine_cos, fine_sin, STEP, 0, 1)
    outer(coarse_cos, coarse_sin, chunks * steps, g * (chunks * chunk), STEP)

    def arrive(k, c):
        wanted = (c >= helped) | jnp.logical_not(edge)

        @pl.when((z - k >= 0) & wanted)
        def _():
            line_copy(z - k, c, 0).wait_recv()

            @pl.when(goes_right(c))
            def _():
                line_copy(z - k, c, 0).start()

        @pl.when((z + k < n) & wanted)
        def _():
            line_copy(z + k, c, 1).wait_recv()

            @pl.when(goes_left(c))
            def _():
                line_copy(z + k, c, 1).start()

    def make_table(c):
        @pl.loop(0, steps)
        def _(i):
            row = c * steps + i
            ca = coarse_cos[pl.ds(row, 1), :]
            sa = coarse_sin[pl.ds(row, 1), :]
            at = pl.multiple_of(c * (2 * chunk) + i * STEP, STEP)
            for r in range(0, STEP, 16):
                cb = fine_cos[r:r + 16, :]
                sb = fine_sin[r:r + 16, :]
                table[pl.ds(at + r, 16), :] = (ca * cb - sa * sb).astype(jnp.bfloat16)
                table[pl.ds(at + chunk + r, 16), :] = -(sa * cb + ca * sb).astype(jnp.bfloat16)

    def compute(w, c):
        origin = jnp.where(w == 0, z, partner)
        own = gathered[c, pl.ds(pl.multiple_of(origin * block, 16), block), :]
        src[...] = jnp.dot(
            picks[w, :, n * block:(n + 1) * block], own, preferred_element_type=jnp.float32
        )
        rcv[...] = jnp.dot(
            picks[w, :, 0:n * block], gathered[c], preferred_element_type=jnp.float32
        )

        @pl.loop(0, groups)
        def _(q):
            base = pl.multiple_of(q * pick_rows, 16)
            top = pl.multiple_of(q * rows, 16)
            for lane in range(0, chunk, 128):
                s = [src[pl.ds(base + pairs * k, pairs), lane:lane + 128] for k in range(6)]
                r = [rcv[pl.ds(base + pairs * k, pairs), lane:lane + 128] for k in range(6)]
                for a in range(3):
                    for b in range(3):
                        spot = pl.ds(top + (3 * a + b) * pairs, pairs)
                        cross[spot, lane:lane + 128] = (s[a] * r[b] + s[3 + a] * r[3 + b]).astype(jnp.bfloat16)
                        cross[spot, chunk + lane:chunk + lane + 128] = (
                            s[a] * r[3 + b] - s[3 + a] * r[b]
                        ).astype(jnp.bfloat16)

        acc[w] += jnp.dot(
            cross[...],
            table[pl.ds(pl.multiple_of(c * (2 * chunk), 16), 2 * chunk), :],
            preferred_element_type=jnp.float32,
        )

    lags = pl.ds(pl.multiple_of(h * part, 128), part)
    own_rows = pl.ds(pl.multiple_of(g * rows, 16), rows)

    def part_copy(w, d):
        t = lax.rem(me + d, plane)
        tg, th = t // hours, lax.rem(t, hours)
        return pltpu.make_async_remote_copy(
            src_ref=partial.at[
                w, pl.ds(pl.multiple_of(tg * rows, 16), rows), pl.ds(pl.multiple_of(th * part, 128), part)
            ],
            dst_ref=landed.at[w, d],
            send_sem=part_send.at[w, d],
            recv_sem=part_recv.at[w, d],
            device_id={"grp": tg, "hr": th},
            device_id_type=MESH,
        )

    def scatter(w):
        partial[w] = acc[w].astype(jnp.bfloat16)

        @pl.loop(1, plane)
        def _(d):
            part_copy(w, d).start()

    def collect(w):
        final[...] = acc[w, own_rows, lags]

        @pl.loop(1, plane)
        def _(d):
            part_copy(w, d).wait_recv()
            final[...] += landed[w, d].astype(jnp.float32)

    def hand_copy():
        return pltpu.make_async_remote_copy(
            src_ref=handed,
            dst_ref=landed.at[0, 0],
            send_sem=hand_send,
            recv_sem=hand_recv,
            device_id={"sta": partner},
            device_id_type=MESH,
        )

    lag_steps = slack * (jnp.maximum(z, n - 1 - z) - 1)

    @pl.loop(0, chunks + slack * max(n - 2, 0))
    def _(it):
        @pl.when(it + ahead < chunks)
        def _():
            send_own(it + ahead)

        @pl.when((it < chunks) & ((it >= helped) | jnp.logical_not(edge)))
        def _():
            make_table(it)

        @pl.loop(1, n)
        def _(k):
            c = it - slack * (k - 1)

            @pl.when((c >= 0) & (c < chunks))
            def _():
                arrive(k, c)

        @pl.when(it == lag_steps)
        def _():
            @pl.loop(1, groups)
            def _(d):
                pick_copy(d).wait()

            if helped:
                @pl.when(helper)
                def _():
                    @pl.loop(0, groups)
                    def _(d):
                        give_copy(d).wait_recv()

        c = it - lag_steps
        turns = jnp.where(c >= helped, 1, jnp.where(edge, 0, jnp.where(helper, 2, 1)))

        @pl.loop(0, jnp.where((c >= 0) & (c < chunks), turns, 0))
        def _(w):
            compute(w, c)

        if helped:
            @pl.when(helper & (c == helped - 1))
            def _():
                scatter(1)

            @pl.when(helper & (c == helped + 1))
            def _():
                collect(1)
                handed[...] = final[...].astype(jnp.bfloat16)
                hand_copy().start()

    scatter(0)
    collect(0)
    if helped:
        @pl.when(edge)
        def _():
            hand_copy().wait_recv()
            final[...] += landed[0, 0].astype(jnp.float32)

    lag = (h * part + lax.broadcasted_iota(jnp.int32, (8, part), 1)).astype(jnp.float32)
    taper = (0.75 - 0.25 * jnp.cos(two_pi * (lag + 0.5) / LAGS)) * scale
    out_ref[:, lags] = (final[...] * taper[0:1, :]).astype(jnp.bfloat16)

    def fin_copy(d):
        return pltpu.make_async_remote_copy(
            src_ref=out_ref.at[:, lags],
            dst_ref=out_ref.at[:, lags],
            send_sem=fin_send.at[d],
            recv_sem=fin_recv.at[d],
            device_id={"hr": lax.rem(h + d, hours)},
            device_id_type=MESH,
        )

    @pl.loop(1, hours)
    def _(d):
        fin_copy(d).start()

    @pl.loop(1, plane)
    def _(d):
        part_copy(0, d).wait_send()

    if helped:
        @pl.when(helper)
        def _():
            hand_copy().wait_send()

            @pl.loop(1, plane)
            def _(d):
                part_copy(1, d).wait_send()

        @pl.when(edge)
        def _():
            @pl.loop(0, groups)
            def _(d):
                give_copy(d).wait_send()

    @pl.loop(0, n - 1)
    def _(k):
        @pl.loop(0, chunks)
        def _(c):
            @pl.when((z - k >= 0) & goes_right(c))
            def _():
                line_copy(z - k, c, 0).wait_send()

            @pl.when((z + k < n) & goes_left(c))
            def _():
                line_copy(z + k, c, 1).wait_send()

    @pl.loop(1, hours)
    def _(d):
        fin_copy(d).wait()


def body(n, groups, hours, spectra, pair_source, pair_owner, pair_row):
    _, sta_dev, comps, num_bins = spectra.shape
    pairs = pair_source.shape[0]
    bins = num_bins // groups
    chunk = min(512, bins)
    chunks = bins // chunk
    helped = 3 * chunks // 8 if n >= 4 else 0
    held = 2 if helped else 1
    block = comps * sta_dev
    pick_rows = comps * pairs
    width = -(-((n + 1) * block) // 128) * 128

    start = lax.axis_index("grp") * bins
    mine = lax.dynamic_slice_in_dim(spectra[0], start, bins, 2)
    spec = jnp.transpose(mine, (1, 0, 2)).reshape(block, bins)

    comp_at = (jnp.arange(comps, dtype=jnp.int32) * sta_dev)[:, None]
    wanted = (comp_at + (pair_owner[:, 0] * block + pair_row)[None, :]).reshape(pick_rows, 1)
    origin = (comp_at + (n * block + pair_source)[None, :]).reshape(pick_rows, 1)
    column = jnp.arange(width, dtype=jnp.int32)[None, :]
    pick = ((wanted == column) | (origin == column)).astype(jnp.bfloat16)

    scale = 1.0 / (hours * spectra.shape[0] * math.sqrt(num_bins))
    rows = 9 * pairs
    plane = groups * hours
    vmem = pl.BlockSpec(memory_space=pltpu.VMEM)
    coarse = pltpu.VMEM((bins // STEP, LAGS), jnp.float32)
    fine = pltpu.VMEM((STEP, LAGS), jnp.float32)
    out = pl.pallas_call(
        functools.partial(kernel, n, groups, hours, pairs, chunk, chunks, helped, 3, 2, scale),
        out_shape=jax.ShapeDtypeStruct((rows, LAGS), jnp.bfloat16),
        in_specs=[vmem, vmem],
        out_specs=vmem,
        scratch_shapes=[
            pltpu.VMEM((chunks, n * block, chunk), jnp.bfloat16),
            pltpu.VMEM((held, groups * pick_rows, width), jnp.bfloat16),
            coarse, coarse, fine, fine,
            pltpu.VMEM((2 * bins, LAGS), jnp.bfloat16),
            pltpu.VMEM((groups * pick_rows, chunk), jnp.float32),
            pltpu.VMEM((groups * pick_rows, chunk), jnp.float32),
            pltpu.VMEM((groups * rows, 2 * chunk), jnp.bfloat16),
            pltpu.VMEM((held, groups * rows, LAGS), jnp.float32),
            pltpu.VMEM((held, groups * rows, LAGS), jnp.bfloat16),
            pltpu.VMEM((held, plane, rows, LAGS // hours), jnp.bfloat16),
            pltpu.VMEM((rows, LAGS // hours), jnp.float32),
            pltpu.VMEM((rows, LAGS // hours), jnp.bfloat16),
            pltpu.SemaphoreType.DMA((2, n, chunks)),
            pltpu.SemaphoreType.DMA((n, chunks)),
            pltpu.SemaphoreType.DMA((groups,)),
            pltpu.SemaphoreType.DMA((groups,)),
            pltpu.SemaphoreType.DMA((groups,)),
            pltpu.SemaphoreType.DMA((groups,)),
            pltpu.SemaphoreType.DMA((held, plane)),
            pltpu.SemaphoreType.DMA((held, plane)),
            pltpu.SemaphoreType.DMA((hours,)),
            pltpu.SemaphoreType.DMA((hours,)),
            pltpu.SemaphoreType.DMA,
            pltpu.SemaphoreType.DMA,
        ],
        compiler_params=pltpu.CompilerParams(
            collective_id=0, has_side_effects=True, vmem_limit_bytes=48 * 1024 * 1024
        ),
        cost_estimate=pl.CostEstimate(
            flops=4 * groups * rows * bins * LAGS, bytes_accessed=4 * block * bins, transcendentals=0
        ),
    )(spec, pick)
    return jnp.transpose(out.reshape(9, pairs, LAGS), (1, 0, 2)).astype(jnp.float32)


def solution(mesh):
    placed = (
        P("hr", "sta", None, None),
        P(("sta", "grp")),
        P(("sta", "grp"), None),
        P(("sta", "grp")),
    )
    sizes = (mesh.shape["sta"], mesh.shape["grp"], mesh.shape["hr"])
    return jax.shard_map(
        functools.partial(body, *sizes),
        mesh=mesh,
        in_specs=placed,
        out_specs=P(("sta", "grp"), None, None),
        check_vma=False,
    )
```

```python
import functools
import math

import jax
import jax.numpy as jnp
import ml_dtypes
import numpy as np
from jax import lax
from jax.experimental import pallas as pl
from jax.experimental.pallas import tpu as pltpu
from jax.sharding import PartitionSpec as P

LAGS = 1024
two_pi = 2.0 * math.pi
MESH = pl.DeviceIdType.MESH


def lag_table(num_bins, chunk):
    period = 2 * num_bins
    shift = np.arange(LAGS) - LAGS // 2
    angles = np.mod(np.arange(num_bins)[:, None] * shift[None, :], period).astype(np.float32) * np.float32(two_pi / period)
    both = np.stack([np.cos(angles), -np.sin(angles)]).reshape(2, num_bins // chunk, chunk, LAGS)
    return both.transpose(1, 0, 2, 3).reshape(2 * num_bins, LAGS).astype(ml_dtypes.bfloat16)


def kernel(
    n, groups, hours, pairs, chunk, chunks, helped, ahead, slack, scale,
    spec_ref, pick_ref, table_ref,
    out_ref,
    gathered, picks, table, src, rcv, cross, acc, partial, landed, final,
    handed,
    send_sem, recv_sem, pick_send, pick_recv, give_send, give_recv, part_send, part_recv, fin_send, fin_recv,
    hand_send, hand_recv, table_sem,
):
    z = lax.axis_index("sta")
    g = lax.axis_index("grp")
    h = lax.axis_index("hr")
    plane = groups * hours
    me = g * hours + h
    block = spec_ref.shape[0]
    pick_rows = pick_ref.shape[0]
    rows = 9 * pairs
    part = LAGS // hours
    edge = (z == 0) | (z == n - 1)
    helper = (z == 1) | (z == n - 2)
    partner = jnp.where(z == 0, 1, jnp.where(z == 1, 0, jnp.where(z == n - 1, n - 2, n - 1)))

    for c in range(chunks):
        gathered[c, pl.ds(pl.multiple_of(z * block, 16), block), :] = spec_ref[:, c * chunk:(c + 1) * chunk]

    def table_copy(c):
        return pltpu.make_async_copy(
            table_ref.at[pl.ds(pl.multiple_of((g * chunks + c) * (2 * chunk), 16), 2 * chunk)],
            table.at[pl.ds(pl.multiple_of(c * (2 * chunk), 16), 2 * chunk)],
            table_sem.at[c],
        )

    barrier = pltpu.get_barrier_semaphore()

    @pl.loop(1, plane)
    def _(d):
        t = lax.rem(me + d, plane)
        pl.semaphore_signal(
            barrier, inc=1, device_id={"grp": t // hours, "hr": lax.rem(t, hours)}, device_id_type=MESH
        )

    @pl.when(z > 0)
    def _():
        pl.semaphore_signal(barrier, inc=1, device_id={"sta": z - 1}, device_id_type=MESH)

    @pl.when(z < n - 1)
    def _():
        pl.semaphore_signal(barrier, inc=1, device_id={"sta": z + 1}, device_id_type=MESH)

    expected = plane - 1 + (z > 0).astype(jnp.int32) + (z < n - 1).astype(jnp.int32)
    if helped:
        @pl.when(edge | helper)
        def _():
            @pl.loop(1, groups)
            def _(d):
                pl.semaphore_signal(
                    barrier, inc=1, device_id={"sta": partner, "grp": lax.rem(g + d, groups)}, device_id_type=MESH
                )

        expected = expected + (groups - 1) * (edge | helper).astype(jnp.int32)
    pl.semaphore_wait(barrier, expected)

    def line_copy(b, c, side):
        spot = gathered.at[c, pl.ds(pl.multiple_of(b * block, 16), block)]
        return pltpu.make_async_remote_copy(
            src_ref=spot,
            dst_ref=spot,
            send_sem=send_sem.at[side, b, c],
            recv_sem=recv_sem.at[b, c],
            device_id={"sta": z + 1 if side == 0 else z - 1},
            device_id_type=MESH,
        )

    def goes_right(c):
        return (z < n - 2) | ((z == n - 2) & (c >= helped))

    def goes_left(c):
        return (z > 1) | ((z == 1) & (c >= helped))

    def send_own(c):
        @pl.when(goes_right(c))
        def _():
            line_copy(z, c, 0).start()

        @pl.when(goes_left(c))
        def _():
            line_copy(z, c, 1).start()

    def pick_copy(d):
        return pltpu.make_async_remote_copy(
            src_ref=pick_ref,
            dst_ref=picks.at[0, pl.ds(pl.multiple_of(g * pick_rows, 16), pick_rows)],
            send_sem=pick_send.at[d],
            recv_sem=pick_recv.at[d],
            device_id={"grp": lax.rem(g + d, groups)},
            device_id_type=MESH,
        )

    def give_copy(d):
        return pltpu.make_async_remote_copy(
            src_ref=pick_ref,
            dst_ref=picks.at[1, pl.ds(pl.multiple_of(g * pick_rows, 16), pick_rows)],
            send_sem=give_send.at[d],
            recv_sem=give_recv.at[d],
            device_id={"sta": partner, "grp": lax.rem(g + d, groups)},
            device_id_type=MESH,
        )

    @pl.loop(0, min(ahead, chunks))
    def _(c):
        send_own(c)

    @pl.loop(0, chunks)
    def _(c):
        table_copy(c).start()

    @pl.loop(1, groups)
    def _(d):
        pick_copy(d).start()

    if helped:
        @pl.when(edge)
        def _():
            @pl.loop(0, groups)
            def _(d):
                give_copy(d).start()

    picks[0, pl.ds(pl.multiple_of(g * pick_rows, 16), pick_rows), :] = pick_ref[...]
    acc[...] = jnp.zeros_like(acc)

    def arrive(k, c):
        wanted = (c >= helped) | jnp.logical_not(edge)

        @pl.when((z - k >= 0) & wanted)
        def _():
            line_copy(z - k, c, 0).wait_recv()

            @pl.when(goes_right(c))
            def _():
                line_copy(z - k, c, 0).start()

        @pl.when((z + k < n) & wanted)
        def _():
            line_copy(z + k, c, 1).wait_recv()

            @pl.when(goes_left(c))
            def _():
                line_copy(z + k, c, 1).start()

    def compute(w, c):
        origin = jnp.where(w == 0, z, partner)
        own = gathered[c, pl.ds(pl.multiple_of(origin * block, 16), block), :]
        src[...] = jnp.dot(
            picks[w, :, n * block:(n + 1) * block], own, preferred_element_type=jnp.float32
        )
        rcv[...] = jnp.dot(
            picks[w, :, 0:n * block], gathered[c], preferred_element_type=jnp.float32
        )

        @pl.loop(0, groups)
        def _(q):
            base = pl.multiple_of(q * pick_rows, 16)
            top = pl.multiple_of(q * rows, 16)
            for lane in range(0, chunk, 128):
                s = [src[pl.ds(base + pairs * k, pairs), lane:lane + 128] for k in range(6)]
                r = [rcv[pl.ds(base + pairs * k, pairs), lane:lane + 128] for k in range(6)]
                for a in range(3):
                    for b in range(3):
                        spot = pl.ds(top + (3 * a + b) * pairs, pairs)
                        cross[spot, lane:lane + 128] = (s[a] * r[b] + s[3 + a] * r[3 + b]).astype(jnp.bfloat16)
                        cross[spot, chunk + lane:chunk + lane + 128] = (
                            s[a] * r[3 + b] - s[3 + a] * r[b]
                        ).astype(jnp.bfloat16)

        acc[w] += jnp.dot(
            cross[...],
            table[pl.ds(pl.multiple_of(c * (2 * chunk), 16), 2 * chunk), :],
            preferred_element_type=jnp.float32,
        )

    lags = pl.ds(pl.multiple_of(h * part, 128), part)
    own_rows = pl.ds(pl.multiple_of(g * rows, 16), rows)

    def part_copy(w, d):
        t = lax.rem(me + d, plane)
        tg, th = t // hours, lax.rem(t, hours)
        return pltpu.make_async_remote_copy(
            src_ref=partial.at[
                w, pl.ds(pl.multiple_of(tg * rows, 16), rows), pl.ds(pl.multiple_of(th * part, 128), part)
            ],
            dst_ref=landed.at[w, d],
            send_sem=part_send.at[w, d],
            recv_sem=part_recv.at[w, d],
            device_id={"grp": tg, "hr": th},
            device_id_type=MESH,
        )

    def scatter(w):
        partial[w] = acc[w].astype(jnp.bfloat16)

        @pl.loop(1, plane)
        def _(d):
            part_copy(w, d).start()

    def collect(w):
        final[...] = acc[w, own_rows, lags]

        @pl.loop(1, plane)
        def _(d):
            part_copy(w, d).wait_recv()
            final[...] += landed[w, d].astype(jnp.float32)

    def hand_copy():
        return pltpu.make_async_remote_copy(
            src_ref=handed,
            dst_ref=landed.at[0, 0],
            send_sem=hand_send,
            recv_sem=hand_recv,
            device_id={"sta": partner},
            device_id_type=MESH,
        )

    lag_steps = slack * (jnp.maximum(z, n - 1 - z) - 1)

    @pl.loop(0, chunks + slack * max(n - 2, 0))
    def _(it):
        @pl.when(it + ahead < chunks)
        def _():
            send_own(it + ahead)

        @pl.loop(1, n)
        def _(k):
            c = it - slack * (k - 1)

            @pl.when((c >= 0) & (c < chunks))
            def _():
                arrive(k, c)

        @pl.when(it == lag_steps)
        def _():
            @pl.loop(1, groups)
            def _(d):
                pick_copy(d).wait()

            if helped:
                @pl.when(helper)
                def _():
                    @pl.loop(0, groups)
                    def _(d):
                        give_copy(d).wait_recv()

        c = it - lag_steps
        @pl.when((c >= 0) & (c < chunks))
        def _():
            table_copy(c).wait()

        turns = jnp.where(c >= helped, 1, jnp.where(edge, 0, jnp.where(helper, 2, 1)))

        @pl.loop(0, jnp.where((c >= 0) & (c < chunks), turns, 0))
        def _(w):
            compute(w, c)

        if helped:
            @pl.when(helper & (c == helped - 1))
            def _():
                scatter(1)

            @pl.when(helper & (c == helped + 1))
            def _():
                collect(1)
                handed[...] = final[...].astype(jnp.bfloat16)
                hand_copy().start()

    scatter(0)
    collect(0)
    if helped:
        @pl.when(edge)
        def _():
            hand_copy().wait_recv()
            final[...] += landed[0, 0].astype(jnp.float32)

    lag = (h * part + lax.broadcasted_iota(jnp.int32, (8, part), 1)).astype(jnp.float32)
    taper = (0.75 - 0.25 * jnp.cos(two_pi * (lag + 0.5) / LAGS)) * scale
    out_ref[:, lags] = (final[...] * taper[0:1, :]).astype(jnp.bfloat16)

    def fin_copy(d):
        return pltpu.make_async_remote_copy(
            src_ref=out_ref.at[:, lags],
            dst_ref=out_ref.at[:, lags],
            send_sem=fin_send.at[d],
            recv_sem=fin_recv.at[d],
            device_id={"hr": lax.rem(h + d, hours)},
            device_id_type=MESH,
        )

    @pl.loop(1, hours)
    def _(d):
        fin_copy(d).start()

    @pl.loop(1, plane)
    def _(d):
        part_copy(0, d).wait_send()

    if helped:
        @pl.when(helper)
        def _():
            hand_copy().wait_send()

            @pl.loop(1, plane)
            def _(d):
                part_copy(1, d).wait_send()

        @pl.when(edge)
        def _():
            @pl.loop(0, groups)
            def _(d):
                give_copy(d).wait_send()

    @pl.loop(0, n - 1)
    def _(k):
        @pl.loop(0, chunks)
        def _(c):
            @pl.when((z - k >= 0) & goes_right(c))
            def _():
                line_copy(z - k, c, 0).wait_send()

            @pl.when((z + k < n) & goes_left(c))
            def _():
                line_copy(z + k, c, 1).wait_send()

    @pl.loop(1, hours)
    def _(d):
        fin_copy(d).wait()


def body(n, groups, hours, spectra, pair_source, pair_owner, pair_row):
    _, sta_dev, comps, num_bins = spectra.shape
    pairs = pair_source.shape[0]
    bins = num_bins // groups
    chunk = min(512, bins)
    chunks = bins // chunk
    helped = 3 * chunks // 8 if n >= 4 else 0
    held = 2 if helped else 1
    block = comps * sta_dev
    pick_rows = comps * pairs
    width = -(-((n + 1) * block) // 128) * 128

    start = lax.axis_index("grp") * bins
    mine = lax.dynamic_slice_in_dim(spectra[0], start, bins, 2)
    spec = jnp.transpose(mine, (1, 0, 2)).reshape(block, bins)

    comp_at = (jnp.arange(comps, dtype=jnp.int32) * sta_dev)[:, None]
    wanted = (comp_at + (pair_owner[:, 0] * block + pair_row)[None, :]).reshape(pick_rows, 1)
    origin = (comp_at + (n * block + pair_source)[None, :]).reshape(pick_rows, 1)
    column = jnp.arange(width, dtype=jnp.int32)[None, :]
    pick = ((wanted == column) | (origin == column)).astype(jnp.bfloat16)

    scale = 1.0 / (hours * spectra.shape[0] * math.sqrt(num_bins))
    rows = 9 * pairs
    plane = groups * hours
    vmem = pl.BlockSpec(memory_space=pltpu.VMEM)
    out = pl.pallas_call(
        functools.partial(kernel, n, groups, hours, pairs, chunk, chunks, helped, 3, 2, scale),
        out_shape=jax.ShapeDtypeStruct((rows, LAGS), jnp.bfloat16),
        in_specs=[vmem, vmem, pl.BlockSpec(memory_space=pltpu.HBM)],
        out_specs=vmem,
        scratch_shapes=[
            pltpu.VMEM((chunks, n * block, chunk), jnp.bfloat16),
            pltpu.VMEM((held, groups * pick_rows, width), jnp.bfloat16),
            pltpu.VMEM((2 * bins, LAGS), jnp.bfloat16),
            pltpu.VMEM((groups * pick_rows, chunk), jnp.float32),
            pltpu.VMEM((groups * pick_rows, chunk), jnp.float32),
            pltpu.VMEM((groups * rows, 2 * chunk), jnp.bfloat16),
            pltpu.VMEM((held, groups * rows, LAGS), jnp.float32),
            pltpu.VMEM((held, groups * rows, LAGS), jnp.bfloat16),
            pltpu.VMEM((held, plane, rows, LAGS // hours), jnp.bfloat16),
            pltpu.VMEM((rows, LAGS // hours), jnp.float32),
            pltpu.VMEM((rows, LAGS // hours), jnp.bfloat16),
            pltpu.SemaphoreType.DMA((2, n, chunks)),
            pltpu.SemaphoreType.DMA((n, chunks)),
            pltpu.SemaphoreType.DMA((groups,)),
            pltpu.SemaphoreType.DMA((groups,)),
            pltpu.SemaphoreType.DMA((groups,)),
            pltpu.SemaphoreType.DMA((groups,)),
            pltpu.SemaphoreType.DMA((held, plane)),
            pltpu.SemaphoreType.DMA((held, plane)),
            pltpu.SemaphoreType.DMA((hours,)),
            pltpu.SemaphoreType.DMA((hours,)),
            pltpu.SemaphoreType.DMA,
            pltpu.SemaphoreType.DMA,
            pltpu.SemaphoreType.DMA((chunks,)),
        ],
        compiler_params=pltpu.CompilerParams(
            collective_id=0, has_side_effects=True, vmem_limit_bytes=48 * 1024 * 1024
        ),
        cost_estimate=pl.CostEstimate(
            flops=4 * groups * rows * bins * LAGS, bytes_accessed=4 * block * bins, transcendentals=0
        ),
    )(spec, pick, jnp.asarray(lag_table(num_bins, chunk)))
    return jnp.transpose(out.reshape(9, pairs, LAGS), (1, 0, 2)).astype(jnp.float32)


def solution(mesh):
    placed = (
        P("hr", "sta", None, None),
        P(("sta", "grp")),
        P(("sta", "grp"), None),
        P(("sta", "grp")),
    )
    sizes = (mesh.shape["sta"], mesh.shape["grp"], mesh.shape["hr"])
    return jax.shard_map(
        functools.partial(body, *sizes),
        mesh=mesh,
        in_specs=placed,
        out_specs=P(("sta", "grp"), None, None),
        check_vma=False,
    )
```

```python
import functools
import math

import jax
import jax.numpy as jnp
import ml_dtypes
import numpy as np
from jax import lax
from jax.experimental import pallas as pl
from jax.experimental.pallas import tpu as pltpu
from jax.sharding import PartitionSpec as P

LAGS = 1024
two_pi = 2.0 * math.pi
MESH = pl.DeviceIdType.MESH


def lag_table(num_bins, chunk):
    period = 2 * num_bins
    shift = np.arange(LAGS) - LAGS // 2
    angles = np.mod(np.arange(num_bins)[:, None] * shift[None, :], period).astype(np.float32) * np.float32(two_pi / period)
    both = np.stack([np.cos(angles), -np.sin(angles)]).reshape(2, num_bins // chunk, chunk, LAGS)
    return both.transpose(1, 0, 2, 3).reshape(2 * num_bins, LAGS).astype(ml_dtypes.bfloat16)


def kernel(
    n, groups, hours, pairs, chunk, chunks, helped, ahead, slack, scale,
    spec_ref, pick_ref, table_ref,
    out_ref,
    gathered, picks, table, src, rcv, cross, acc, partial, paired, mid, landed, final,
    handed,
    send_sem, recv_sem, pick_send, pick_recv, give_send, give_recv, pair_send, pair_recv, part_send, part_recv, fin_send, fin_recv,
    hand_send, hand_recv, table_sem,
):
    z = lax.axis_index("sta")
    g = lax.axis_index("grp")
    h = lax.axis_index("hr")
    plane = groups * hours
    me = g * hours + h
    block = spec_ref.shape[0]
    pick_rows = pick_ref.shape[0]
    rows = 9 * pairs
    part = LAGS // hours
    edge = (z == 0) | (z == n - 1)
    helper = (z == 1) | (z == n - 2)
    partner = jnp.where(z == 0, 1, jnp.where(z == 1, 0, jnp.where(z == n - 1, n - 2, n - 1)))

    for c in range(chunks):
        gathered[c, pl.ds(pl.multiple_of(z * block, 16), block), :] = spec_ref[:, c * chunk:(c + 1) * chunk]

    def table_copy(c):
        return pltpu.make_async_copy(
            table_ref.at[pl.ds(pl.multiple_of((g * chunks + c) * (2 * chunk), 16), 2 * chunk)],
            table.at[pl.ds(pl.multiple_of(c * (2 * chunk), 16), 2 * chunk)],
            table_sem.at[c],
        )

    barrier = pltpu.get_barrier_semaphore()

    @pl.loop(1, plane)
    def _(d):
        t = lax.rem(me + d, plane)
        pl.semaphore_signal(
            barrier, inc=1, device_id={"grp": t // hours, "hr": lax.rem(t, hours)}, device_id_type=MESH
        )

    @pl.when(z > 0)
    def _():
        pl.semaphore_signal(barrier, inc=1, device_id={"sta": z - 1}, device_id_type=MESH)

    @pl.when(z < n - 1)
    def _():
        pl.semaphore_signal(barrier, inc=1, device_id={"sta": z + 1}, device_id_type=MESH)

    expected = plane - 1 + (z > 0).astype(jnp.int32) + (z < n - 1).astype(jnp.int32)
    if helped:
        @pl.when(edge | helper)
        def _():
            @pl.loop(1, groups)
            def _(d):
                pl.semaphore_signal(
                    barrier, inc=1, device_id={"sta": partner, "grp": lax.rem(g + d, groups)}, device_id_type=MESH
                )

        expected = expected + (groups - 1) * (edge | helper).astype(jnp.int32)
    pl.semaphore_wait(barrier, expected)

    def line_copy(b, c, side):
        spot = gathered.at[c, pl.ds(pl.multiple_of(b * block, 16), block)]
        return pltpu.make_async_remote_copy(
            src_ref=spot,
            dst_ref=spot,
            send_sem=send_sem.at[side, b, c],
            recv_sem=recv_sem.at[b, c],
            device_id={"sta": z + 1 if side == 0 else z - 1},
            device_id_type=MESH,
        )

    def goes_right(c):
        return (z < n - 2) | ((z == n - 2) & (c >= helped))

    def goes_left(c):
        return (z > 1) | ((z == 1) & (c >= helped))

    def send_own(c):
        @pl.when(goes_right(c))
        def _():
            line_copy(z, c, 0).start()

        @pl.when(goes_left(c))
        def _():
            line_copy(z, c, 1).start()

    def pick_copy(d):
        return pltpu.make_async_remote_copy(
            src_ref=pick_ref,
            dst_ref=picks.at[0, pl.ds(pl.multiple_of(g * pick_rows, 16), pick_rows)],
            send_sem=pick_send.at[d],
            recv_sem=pick_recv.at[d],
            device_id={"grp": lax.rem(g + d, groups)},
            device_id_type=MESH,
        )

    def give_copy(d):
        return pltpu.make_async_remote_copy(
            src_ref=pick_ref,
            dst_ref=picks.at[1, pl.ds(pl.multiple_of(g * pick_rows, 16), pick_rows)],
            send_sem=give_send.at[d],
            recv_sem=give_recv.at[d],
            device_id={"sta": partner, "grp": lax.rem(g + d, groups)},
            device_id_type=MESH,
        )

    @pl.loop(0, min(ahead, chunks))
    def _(c):
        send_own(c)

    @pl.loop(0, chunks)
    def _(c):
        table_copy(c).start()

    @pl.loop(1, groups)
    def _(d):
        pick_copy(d).start()

    if helped:
        @pl.when(edge)
        def _():
            @pl.loop(0, groups)
            def _(d):
                give_copy(d).start()

    picks[0, pl.ds(pl.multiple_of(g * pick_rows, 16), pick_rows), :] = pick_ref[...]
    acc[...] = jnp.zeros_like(acc)

    def arrive(k, c):
        wanted = (c >= helped) | jnp.logical_not(edge)

        @pl.when((z - k >= 0) & wanted)
        def _():
            line_copy(z - k, c, 0).wait_recv()

            @pl.when(goes_right(c))
            def _():
                line_copy(z - k, c, 0).start()

        @pl.when((z + k < n) & wanted)
        def _():
            line_copy(z + k, c, 1).wait_recv()

            @pl.when(goes_left(c))
            def _():
                line_copy(z + k, c, 1).start()

    def compute(w, c):
        origin = jnp.where(w == 0, z, partner)
        own = gathered[c, pl.ds(pl.multiple_of(origin * block, 16), block), :]
        src[...] = jnp.dot(
            picks[w, :, n * block:(n + 1) * block], own, preferred_element_type=jnp.float32
        )
        rcv[...] = jnp.dot(
            picks[w, :, 0:n * block], gathered[c], preferred_element_type=jnp.float32
        )

        @pl.loop(0, groups)
        def _(q):
            base = pl.multiple_of(q * pick_rows, 16)
            top = pl.multiple_of(q * rows, 16)
            for lane in range(0, chunk, 128):
                s = [src[pl.ds(base + pairs * k, pairs), lane:lane + 128] for k in range(6)]
                r = [rcv[pl.ds(base + pairs * k, pairs), lane:lane + 128] for k in range(6)]
                for a in range(3):
                    for b in range(3):
                        spot = pl.ds(top + (3 * a + b) * pairs, pairs)
                        cross[spot, lane:lane + 128] = (s[a] * r[b] + s[3 + a] * r[3 + b]).astype(jnp.bfloat16)
                        cross[spot, chunk + lane:chunk + lane + 128] = (
                            s[a] * r[3 + b] - s[3 + a] * r[b]
                        ).astype(jnp.bfloat16)

        acc[w] += jnp.dot(
            cross[...],
            table[pl.ds(pl.multiple_of(c * (2 * chunk), 16), 2 * chunk), :],
            preferred_element_type=jnp.float32,
        )

    quads = hours // 2
    q, odd = h // 2, lax.rem(h, 2)
    half = quads * part
    my_half = pl.ds(pl.multiple_of(odd * half, 128), half)
    other_half = pl.ds(pl.multiple_of((1 - odd) * half, 128), half)
    in_half = pl.ds(pl.multiple_of(q * part, 128), part)
    lag_start = odd * half + q * part
    lags = pl.ds(pl.multiple_of(lag_start, 128), part)
    own_rows = pl.ds(pl.multiple_of(g * rows, 16), rows)
    owners = groups * quads

    def pair_copy(w):
        return pltpu.make_async_remote_copy(
            src_ref=partial.at[w],
            dst_ref=paired.at[w],
            send_sem=pair_send.at[w],
            recv_sem=pair_recv.at[w],
            device_id={"hr": 2 * q + (1 - odd)},
            device_id_type=MESH,
        )

    def part_copy(w, d):
        t = lax.rem(g * quads + q + d, owners)
        tg, tq = t // quads, lax.rem(t, quads)
        return pltpu.make_async_remote_copy(
            src_ref=mid.at[
                w, pl.ds(pl.multiple_of(tg * rows, 16), rows), pl.ds(pl.multiple_of(tq * part, 128), part)
            ],
            dst_ref=landed.at[w, d],
            send_sem=part_send.at[w, d],
            recv_sem=part_recv.at[w, d],
            device_id={"grp": tg, "hr": 2 * tq + odd},
            device_id_type=MESH,
        )

    def pair_up(w):
        partial[w] = acc[w, :, other_half].astype(jnp.bfloat16)
        pair_copy(w).start()

    def scatter(w):
        pair_copy(w).wait_recv()
        mid[w] = (acc[w, :, my_half] + paired[w].astype(jnp.float32)).astype(jnp.bfloat16)

        @pl.loop(1, owners)
        def _(d):
            part_copy(w, d).start()

    def collect(w):
        final[...] = acc[w, own_rows, lags] + paired[w, own_rows, in_half].astype(jnp.float32)

        @pl.loop(1, owners)
        def _(d):
            part_copy(w, d).wait_recv()
            final[...] += landed[w, d].astype(jnp.float32)

    def hand_copy():
        return pltpu.make_async_remote_copy(
            src_ref=handed,
            dst_ref=landed.at[0, 0],
            send_sem=hand_send,
            recv_sem=hand_recv,
            device_id={"sta": partner},
            device_id_type=MESH,
        )

    lag_steps = slack * (jnp.maximum(z, n - 1 - z) - 1)

    @pl.loop(0, chunks + slack * max(n - 2, 0))
    def _(it):
        @pl.when(it + ahead < chunks)
        def _():
            send_own(it + ahead)

        @pl.loop(1, n)
        def _(k):
            c = it - slack * (k - 1)

            @pl.when((c >= 0) & (c < chunks))
            def _():
                arrive(k, c)

        @pl.when(it == lag_steps)
        def _():
            @pl.loop(1, groups)
            def _(d):
                pick_copy(d).wait()

            if helped:
                @pl.when(helper)
                def _():
                    @pl.loop(0, groups)
                    def _(d):
                        give_copy(d).wait_recv()

        c = it - lag_steps
        @pl.when((c >= 0) & (c < chunks))
        def _():
            table_copy(c).wait()

        turns = jnp.where(c >= helped, 1, jnp.where(edge, 0, jnp.where(helper, 2, 1)))

        @pl.loop(0, jnp.where((c >= 0) & (c < chunks), turns, 0))
        def _(w):
            compute(w, c)

        if helped:
            @pl.when(helper & (c == helped - 1))
            def _():
                pair_up(1)

            @pl.when(helper & (c == helped))
            def _():
                scatter(1)

    pair_up(0)
    if helped:
        @pl.when(helper)
        def _():
            collect(1)
            handed[...] = final[...].astype(jnp.bfloat16)
            hand_copy().start()

    scatter(0)
    collect(0)
    if helped:
        @pl.when(edge)
        def _():
            hand_copy().wait_recv()
            final[...] += landed[0, 0].astype(jnp.float32)

    lag = (lag_start + lax.broadcasted_iota(jnp.int32, (8, part), 1)).astype(jnp.float32)
    taper = (0.75 - 0.25 * jnp.cos(two_pi * (lag + 0.5) / LAGS)) * scale
    out_ref[:, lags] = (final[...] * taper[0:1, :]).astype(jnp.bfloat16)

    def fin_copy(d):
        return pltpu.make_async_remote_copy(
            src_ref=out_ref.at[:, lags],
            dst_ref=out_ref.at[:, lags],
            send_sem=fin_send.at[d],
            recv_sem=fin_recv.at[d],
            device_id={"hr": lax.rem(h + d, hours)},
            device_id_type=MESH,
        )

    @pl.loop(1, hours)
    def _(d):
        fin_copy(d).start()

    pair_copy(0).wait_send()

    @pl.loop(1, owners)
    def _(d):
        part_copy(0, d).wait_send()

    if helped:
        @pl.when(helper)
        def _():
            hand_copy().wait_send()
            pair_copy(1).wait_send()

            @pl.loop(1, owners)
            def _(d):
                part_copy(1, d).wait_send()

        @pl.when(edge)
        def _():
            @pl.loop(0, groups)
            def _(d):
                give_copy(d).wait_send()

    @pl.loop(0, n - 1)
    def _(k):
        @pl.loop(0, chunks)
        def _(c):
            @pl.when((z - k >= 0) & goes_right(c))
            def _():
                line_copy(z - k, c, 0).wait_send()

            @pl.when((z + k < n) & goes_left(c))
            def _():
                line_copy(z + k, c, 1).wait_send()

    @pl.loop(1, hours)
    def _(d):
        fin_copy(d).wait()


def body(n, groups, hours, spectra, pair_source, pair_owner, pair_row):
    _, sta_dev, comps, num_bins = spectra.shape
    pairs = pair_source.shape[0]
    bins = num_bins // groups
    chunk = min(512, bins)
    chunks = bins // chunk
    helped = 3 * chunks // 8 if n >= 4 else 0
    held = 2 if helped else 1
    block = comps * sta_dev
    pick_rows = comps * pairs
    width = -(-((n + 1) * block) // 128) * 128

    start = lax.axis_index("grp") * bins
    mine = lax.dynamic_slice_in_dim(spectra[0], start, bins, 2)
    spec = jnp.transpose(mine, (1, 0, 2)).reshape(block, bins)

    comp_at = (jnp.arange(comps, dtype=jnp.int32) * sta_dev)[:, None]
    wanted = (comp_at + (pair_owner[:, 0] * block + pair_row)[None, :]).reshape(pick_rows, 1)
    origin = (comp_at + (n * block + pair_source)[None, :]).reshape(pick_rows, 1)
    column = jnp.arange(width, dtype=jnp.int32)[None, :]
    pick = ((wanted == column) | (origin == column)).astype(jnp.bfloat16)

    scale = 1.0 / (hours * spectra.shape[0] * math.sqrt(num_bins))
    rows = 9 * pairs
    vmem = pl.BlockSpec(memory_space=pltpu.VMEM)
    out = pl.pallas_call(
        functools.partial(kernel, n, groups, hours, pairs, chunk, chunks, helped, 3, 2, scale),
        out_shape=jax.ShapeDtypeStruct((rows, LAGS), jnp.bfloat16),
        in_specs=[vmem, vmem, pl.BlockSpec(memory_space=pltpu.HBM)],
        out_specs=vmem,
        scratch_shapes=[
            pltpu.VMEM((chunks, n * block, chunk), jnp.bfloat16),
            pltpu.VMEM((held, groups * pick_rows, width), jnp.bfloat16),
            pltpu.VMEM((2 * bins, LAGS), jnp.bfloat16),
            pltpu.VMEM((groups * pick_rows, chunk), jnp.float32),
            pltpu.VMEM((groups * pick_rows, chunk), jnp.float32),
            pltpu.VMEM((groups * rows, 2 * chunk), jnp.bfloat16),
            pltpu.VMEM((held, groups * rows, LAGS), jnp.float32),
            pltpu.VMEM((held, groups * rows, LAGS // 2), jnp.bfloat16),
            pltpu.VMEM((held, groups * rows, LAGS // 2), jnp.bfloat16),
            pltpu.VMEM((held, groups * rows, LAGS // 2), jnp.bfloat16),
            pltpu.VMEM((held, groups * hours // 2, rows, LAGS // hours), jnp.bfloat16),
            pltpu.VMEM((rows, LAGS // hours), jnp.float32),
            pltpu.VMEM((rows, LAGS // hours), jnp.bfloat16),
            pltpu.SemaphoreType.DMA((2, n, chunks)),
            pltpu.SemaphoreType.DMA((n, chunks)),
            pltpu.SemaphoreType.DMA((groups,)),
            pltpu.SemaphoreType.DMA((groups,)),
            pltpu.SemaphoreType.DMA((groups,)),
            pltpu.SemaphoreType.DMA((groups,)),
            pltpu.SemaphoreType.DMA((held,)),
            pltpu.SemaphoreType.DMA((held,)),
            pltpu.SemaphoreType.DMA((held, groups * hours // 2)),
            pltpu.SemaphoreType.DMA((held, groups * hours // 2)),
            pltpu.SemaphoreType.DMA((hours,)),
            pltpu.SemaphoreType.DMA((hours,)),
            pltpu.SemaphoreType.DMA,
            pltpu.SemaphoreType.DMA,
            pltpu.SemaphoreType.DMA((chunks,)),
        ],
        compiler_params=pltpu.CompilerParams(
            collective_id=0, has_side_effects=True, vmem_limit_bytes=48 * 1024 * 1024
        ),
        cost_estimate=pl.CostEstimate(
            flops=4 * groups * rows * bins * LAGS, bytes_accessed=4 * block * bins, transcendentals=0
        ),
    )(spec, pick, jnp.asarray(lag_table(num_bins, chunk)))
    return jnp.transpose(out.reshape(9, pairs, LAGS), (1, 0, 2)).astype(jnp.float32)


def solution(mesh):
    placed = (
        P("hr", "sta", None, None),
        P(("sta", "grp")),
        P(("sta", "grp"), None),
        P(("sta", "grp")),
    )
    sizes = (mesh.shape["sta"], mesh.shape["grp"], mesh.shape["hr"])
    return jax.shard_map(
        functools.partial(body, *sizes),
        mesh=mesh,
        in_specs=placed,
        out_specs=P(("sta", "grp"), None, None),
        check_vma=False,
    )
```

```python
import functools
import math

import jax
import jax.numpy as jnp
import ml_dtypes
import numpy as np
from jax import lax
from jax.experimental import pallas as pl
from jax.experimental.pallas import tpu as pltpu
from jax.sharding import PartitionSpec as P

LAGS = 1024
two_pi = 2.0 * math.pi
MESH = pl.DeviceIdType.MESH


def lag_table(num_bins, chunk):
    period = 2 * num_bins
    shift = np.arange(LAGS) - LAGS // 2
    angles = np.mod(np.arange(num_bins)[:, None] * shift[None, :], period).astype(np.float32) * np.float32(two_pi / period)
    both = np.stack([np.cos(angles), -np.sin(angles)]).reshape(2, num_bins // chunk, chunk, LAGS)
    return both.transpose(1, 0, 2, 3).reshape(2 * num_bins, LAGS).astype(ml_dtypes.bfloat16)


def kernel(
    n, groups, hours, pairs, chunk, chunks, helped, ahead, slack, scale,
    spec_ref, pick_ref, table_ref,
    out_ref,
    gathered, picks, table, src, rcv, cross, acc, partial, paired, mid, landed, final,
    handed,
    send_sem, recv_sem, pick_send, pick_recv, give_send, give_recv, pair_send, pair_recv, part_send, part_recv, fin_send, fin_recv,
    hand_send, hand_recv, table_sem,
):
    z = lax.axis_index("sta")
    g = lax.axis_index("grp")
    h = lax.axis_index("hr")
    plane = groups * hours
    me = g * hours + h
    block = spec_ref.shape[0]
    pick_rows = pick_ref.shape[0]
    rows = 9 * pairs
    part = LAGS // hours
    edge = (z == 0) | (z == n - 1)
    helper = (z == 1) | (z == n - 2)
    partner = jnp.where(z == 0, 1, jnp.where(z == 1, 0, jnp.where(z == n - 1, n - 2, n - 1)))

    for c in range(chunks):
        gathered[c, pl.ds(pl.multiple_of(z * block, 16), block), :] = spec_ref[:, c * chunk:(c + 1) * chunk]

    def table_copy(c):
        return pltpu.make_async_copy(
            table_ref.at[pl.ds(pl.multiple_of((g * chunks + c) * (2 * chunk), 16), 2 * chunk)],
            table.at[pl.ds(pl.multiple_of(c * (2 * chunk), 16), 2 * chunk)],
            table_sem.at[c],
        )

    barrier = pltpu.get_barrier_semaphore()

    @pl.loop(1, plane)
    def _(d):
        t = lax.rem(me + d, plane)
        pl.semaphore_signal(
            barrier, inc=1, device_id={"grp": t // hours, "hr": lax.rem(t, hours)}, device_id_type=MESH
        )

    @pl.when(z > 0)
    def _():
        pl.semaphore_signal(barrier, inc=1, device_id={"sta": z - 1}, device_id_type=MESH)

    @pl.when(z < n - 1)
    def _():
        pl.semaphore_signal(barrier, inc=1, device_id={"sta": z + 1}, device_id_type=MESH)

    expected = plane - 1 + (z > 0).astype(jnp.int32) + (z < n - 1).astype(jnp.int32)
    if helped:
        @pl.when(edge | helper)
        def _():
            @pl.loop(1, groups)
            def _(d):
                pl.semaphore_signal(
                    barrier, inc=1, device_id={"sta": partner, "grp": lax.rem(g + d, groups)}, device_id_type=MESH
                )

        expected = expected + (groups - 1) * (edge | helper).astype(jnp.int32)
    pl.semaphore_wait(barrier, expected)

    def line_copy(b, c, side):
        spot = gathered.at[c, pl.ds(pl.multiple_of(b * block, 16), block)]
        return pltpu.make_async_remote_copy(
            src_ref=spot,
            dst_ref=spot,
            send_sem=send_sem.at[side, b, c],
            recv_sem=recv_sem.at[b, c],
            device_id={"sta": z + 1 if side == 0 else z - 1},
            device_id_type=MESH,
        )

    def goes_right(c):
        return (z < n - 2) | ((z == n - 2) & (c >= helped))

    def goes_left(c):
        return (z > 1) | ((z == 1) & (c >= helped))

    def send_own(c):
        @pl.when(goes_right(c))
        def _():
            line_copy(z, c, 0).start()

        @pl.when(goes_left(c))
        def _():
            line_copy(z, c, 1).start()

    def pick_copy(d):
        return pltpu.make_async_remote_copy(
            src_ref=pick_ref,
            dst_ref=picks.at[0, pl.ds(pl.multiple_of(g * pick_rows, 16), pick_rows)],
            send_sem=pick_send.at[d],
            recv_sem=pick_recv.at[d],
            device_id={"grp": lax.rem(g + d, groups)},
            device_id_type=MESH,
        )

    def give_copy(d):
        return pltpu.make_async_remote_copy(
            src_ref=pick_ref,
            dst_ref=picks.at[1, pl.ds(pl.multiple_of(g * pick_rows, 16), pick_rows)],
            send_sem=give_send.at[d],
            recv_sem=give_recv.at[d],
            device_id={"sta": partner, "grp": lax.rem(g + d, groups)},
            device_id_type=MESH,
        )

    @pl.loop(0, min(ahead, chunks))
    def _(c):
        send_own(c)

    @pl.loop(0, chunks)
    def _(c):
        table_copy(c).start()

    @pl.loop(1, groups)
    def _(d):
        pick_copy(d).start()

    if helped:
        @pl.when(edge)
        def _():
            @pl.loop(0, groups)
            def _(d):
                give_copy(d).start()

    picks[0, pl.ds(pl.multiple_of(g * pick_rows, 16), pick_rows), :] = pick_ref[...]
    acc[...] = jnp.zeros_like(acc)

    def arrive(k, c):
        wanted = (c >= helped) | jnp.logical_not(edge)

        @pl.when((z - k >= 0) & wanted)
        def _():
            line_copy(z - k, c, 0).wait_recv()

            @pl.when(goes_right(c))
            def _():
                line_copy(z - k, c, 0).start()

        @pl.when((z + k < n) & wanted)
        def _():
            line_copy(z + k, c, 1).wait_recv()

            @pl.when(goes_left(c))
            def _():
                line_copy(z + k, c, 1).start()

    def compute(w, c):
        origin = jnp.where(w == 0, z, partner)
        own = gathered[c, pl.ds(pl.multiple_of(origin * block, 16), block), :]
        src[...] = jnp.dot(
            picks[w, :, n * block:(n + 1) * block], own, preferred_element_type=jnp.float32
        )
        rcv[...] = jnp.dot(
            picks[w, :, 0:n * block], gathered[c], preferred_element_type=jnp.float32
        )

        @pl.loop(0, groups)
        def _(q):
            base = pl.multiple_of(q * pick_rows, 16)
            top = pl.multiple_of(q * rows, 16)
            for lane in range(0, chunk, 128):
                s = [src[pl.ds(base + pairs * k, pairs), lane:lane + 128] for k in range(6)]
                r = [rcv[pl.ds(base + pairs * k, pairs), lane:lane + 128] for k in range(6)]
                for a in range(3):
                    for b in range(3):
                        spot = pl.ds(top + (3 * a + b) * pairs, pairs)
                        cross[spot, lane:lane + 128] = (s[a] * r[b] + s[3 + a] * r[3 + b]).astype(jnp.bfloat16)
                        cross[spot, chunk + lane:chunk + lane + 128] = (
                            s[a] * r[3 + b] - s[3 + a] * r[b]
                        ).astype(jnp.bfloat16)

        acc[w] += jnp.dot(
            cross[...],
            table[pl.ds(pl.multiple_of(c * (2 * chunk), 16), 2 * chunk), :],
            preferred_element_type=jnp.float32,
        )

    quads = hours // 2
    q, odd = h // 2, lax.rem(h, 2)
    half = quads * part
    my_half = pl.ds(pl.multiple_of(odd * half, 128), half)
    other_half = pl.ds(pl.multiple_of((1 - odd) * half, 128), half)
    in_half = pl.ds(pl.multiple_of(q * part, 128), part)
    lag_start = odd * half + q * part
    lags = pl.ds(pl.multiple_of(lag_start, 128), part)
    own_rows = pl.ds(pl.multiple_of(g * rows, 16), rows)
    owners = groups * quads

    def pair_copy(w):
        return pltpu.make_async_remote_copy(
            src_ref=partial.at[w],
            dst_ref=paired.at[w],
            send_sem=pair_send.at[w],
            recv_sem=pair_recv.at[w],
            device_id={"hr": 2 * q + (1 - odd)},
            device_id_type=MESH,
        )

    def part_copy(w, d):
        t = lax.rem(g * quads + q + d, owners)
        tg, tq = t // quads, lax.rem(t, quads)
        return pltpu.make_async_remote_copy(
            src_ref=mid.at[
                w, pl.ds(pl.multiple_of(tg * rows, 16), rows), pl.ds(pl.multiple_of(tq * part, 128), part)
            ],
            dst_ref=landed.at[w, d],
            send_sem=part_send.at[w, d],
            recv_sem=part_recv.at[w, d],
            device_id={"grp": tg, "hr": 2 * tq + odd},
            device_id_type=MESH,
        )

    def pair_up(w):
        partial[w] = acc[w, :, other_half].astype(jnp.bfloat16)
        pair_copy(w).start()

    def scatter(w):
        pair_copy(w).wait_recv()
        mid[w] = (acc[w, :, my_half] + paired[w].astype(jnp.float32)).astype(jnp.bfloat16)

        @pl.loop(1, owners)
        def _(d):
            part_copy(w, d).start()

    def collect(w):
        final[...] = acc[w, own_rows, lags] + paired[w, own_rows, in_half].astype(jnp.float32)

        @pl.loop(1, owners)
        def _(d):
            part_copy(w, d).wait_recv()
            final[...] += landed[w, d].astype(jnp.float32)

    def hand_copy():
        return pltpu.make_async_remote_copy(
            src_ref=handed,
            dst_ref=landed.at[0, 0],
            send_sem=hand_send,
            recv_sem=hand_recv,
            device_id={"sta": partner},
            device_id_type=MESH,
        )

    lag_steps = slack * (jnp.maximum(z, n - 1 - z) - 1)

    @pl.loop(0, chunks + slack * max(n - 2, 0))
    def _(it):
        @pl.when(it + ahead < chunks)
        def _():
            send_own(it + ahead)

        @pl.loop(1, n)
        def _(k):
            c = it - slack * (k - 1)

            @pl.when((c >= 0) & (c < chunks))
            def _():
                arrive(k, c)

        @pl.when(it == lag_steps)
        def _():
            @pl.loop(1, groups)
            def _(d):
                pick_copy(d).wait()

            if helped:
                @pl.when(helper)
                def _():
                    @pl.loop(0, groups)
                    def _(d):
                        give_copy(d).wait_recv()

        c = it - lag_steps
        @pl.when((c >= 0) & (c < chunks))
        def _():
            table_copy(c).wait()

        turns = jnp.where(c >= helped, 1, jnp.where(edge, 0, jnp.where(helper, 2, 1)))

        @pl.loop(0, jnp.where((c >= 0) & (c < chunks), turns, 0))
        def _(w):
            compute(w, c)

        if helped:
            @pl.when(helper & (c == helped - 1))
            def _():
                pair_up(1)

            @pl.when(helper & (c == helped))
            def _():
                scatter(1)

    pair_up(0)
    if helped:
        @pl.when(helper)
        def _():
            collect(1)
            handed[...] = final[...].astype(jnp.bfloat16)
            hand_copy().start()

    scatter(0)
    collect(0)
    if helped:
        @pl.when(edge)
        def _():
            hand_copy().wait_recv()
            final[...] += landed[0, 0].astype(jnp.float32)

    lag = (lag_start + lax.broadcasted_iota(jnp.int32, (8, part), 1)).astype(jnp.float32)
    taper = (0.75 - 0.25 * jnp.cos(two_pi * (lag + 0.5) / LAGS)) * scale
    out_ref[:, lags] = (final[...] * taper[0:1, :]).astype(jnp.bfloat16)

    def fin_copy(d):
        return pltpu.make_async_remote_copy(
            src_ref=out_ref.at[:, lags],
            dst_ref=out_ref.at[:, lags],
            send_sem=fin_send.at[d],
            recv_sem=fin_recv.at[d],
            device_id={"hr": lax.rem(h + d, hours)},
            device_id_type=MESH,
        )

    @pl.loop(1, hours)
    def _(d):
        fin_copy(d).start()

    pair_copy(0).wait_send()

    @pl.loop(1, owners)
    def _(d):
        part_copy(0, d).wait_send()

    if helped:
        @pl.when(helper)
        def _():
            hand_copy().wait_send()
            pair_copy(1).wait_send()

            @pl.loop(1, owners)
            def _(d):
                part_copy(1, d).wait_send()

        @pl.when(edge)
        def _():
            @pl.loop(0, groups)
            def _(d):
                give_copy(d).wait_send()

    @pl.loop(0, n - 1)
    def _(k):
        @pl.loop(0, chunks)
        def _(c):
            @pl.when((z - k >= 0) & goes_right(c))
            def _():
                line_copy(z - k, c, 0).wait_send()

            @pl.when((z + k < n) & goes_left(c))
            def _():
                line_copy(z + k, c, 1).wait_send()

    @pl.loop(1, hours)
    def _(d):
        fin_copy(d).wait()


def body(n, groups, hours, spectra, pair_source, pair_owner, pair_row):
    _, sta_dev, comps, num_bins = spectra.shape
    pairs = pair_source.shape[0]
    bins = num_bins // groups
    chunk = min(256, bins)
    chunks = bins // chunk
    helped = 5 * chunks // 16 if n >= 4 else 0
    held = 2 if helped else 1
    block = comps * sta_dev
    pick_rows = comps * pairs
    width = -(-((n + 1) * block) // 128) * 128

    start = lax.axis_index("grp") * bins
    mine = lax.dynamic_slice_in_dim(spectra[0], start, bins, 2)
    spec = jnp.transpose(mine, (1, 0, 2)).reshape(block, bins)

    comp_at = (jnp.arange(comps, dtype=jnp.int32) * sta_dev)[:, None]
    wanted = (comp_at + (pair_owner[:, 0] * block + pair_row)[None, :]).reshape(pick_rows, 1)
    origin = (comp_at + (n * block + pair_source)[None, :]).reshape(pick_rows, 1)
    column = jnp.arange(width, dtype=jnp.int32)[None, :]
    pick = ((wanted == column) | (origin == column)).astype(jnp.bfloat16)

    scale = 1.0 / (hours * spectra.shape[0] * math.sqrt(num_bins))
    rows = 9 * pairs
    vmem = pl.BlockSpec(memory_space=pltpu.VMEM)
    out = pl.pallas_call(
        functools.partial(kernel, n, groups, hours, pairs, chunk, chunks, helped, 6, 2, scale),
        out_shape=jax.ShapeDtypeStruct((rows, LAGS), jnp.bfloat16),
        in_specs=[vmem, vmem, pl.BlockSpec(memory_space=pltpu.HBM)],
        out_specs=vmem,
        scratch_shapes=[
            pltpu.VMEM((chunks, n * block, chunk), jnp.bfloat16),
            pltpu.VMEM((held, groups * pick_rows, width), jnp.bfloat16),
            pltpu.VMEM((2 * bins, LAGS), jnp.bfloat16),
            pltpu.VMEM((groups * pick_rows, chunk), jnp.float32),
            pltpu.VMEM((groups * pick_rows, chunk), jnp.float32),
            pltpu.VMEM((groups * rows, 2 * chunk), jnp.bfloat16),
            pltpu.VMEM((held, groups * rows, LAGS), jnp.float32),
            pltpu.VMEM((held, groups * rows, LAGS // 2), jnp.bfloat16),
            pltpu.VMEM((held, groups * rows, LAGS // 2), jnp.bfloat16),
            pltpu.VMEM((held, groups * rows, LAGS // 2), jnp.bfloat16),
            pltpu.VMEM((held, groups * hours // 2, rows, LAGS // hours), jnp.bfloat16),
            pltpu.VMEM((rows, LAGS // hours), jnp.float32),
            pltpu.VMEM((rows, LAGS // hours), jnp.bfloat16),
            pltpu.SemaphoreType.DMA((2, n, chunks)),
            pltpu.SemaphoreType.DMA((n, chunks)),
            pltpu.SemaphoreType.DMA((groups,)),
            pltpu.SemaphoreType.DMA((groups,)),
            pltpu.SemaphoreType.DMA((groups,)),
            pltpu.SemaphoreType.DMA((groups,)),
            pltpu.SemaphoreType.DMA((held,)),
            pltpu.SemaphoreType.DMA((held,)),
            pltpu.SemaphoreType.DMA((held, groups * hours // 2)),
            pltpu.SemaphoreType.DMA((held, groups * hours // 2)),
            pltpu.SemaphoreType.DMA((hours,)),
            pltpu.SemaphoreType.DMA((hours,)),
            pltpu.SemaphoreType.DMA,
            pltpu.SemaphoreType.DMA,
            pltpu.SemaphoreType.DMA((chunks,)),
        ],
        compiler_params=pltpu.CompilerParams(
            collective_id=0, has_side_effects=True, vmem_limit_bytes=48 * 1024 * 1024
        ),
        cost_estimate=pl.CostEstimate(
            flops=4 * groups * rows * bins * LAGS, bytes_accessed=4 * block * bins, transcendentals=0
        ),
    )(spec, pick, jnp.asarray(lag_table(num_bins, chunk)))
    return jnp.transpose(out.reshape(9, pairs, LAGS), (1, 0, 2)).astype(jnp.float32)


def solution(mesh):
    placed = (
        P("hr", "sta", None, None),
        P(("sta", "grp")),
        P(("sta", "grp"), None),
        P(("sta", "grp")),
    )
    sizes = (mesh.shape["sta"], mesh.shape["grp"], mesh.shape["hr"])
    return jax.shard_map(
        functools.partial(body, *sizes),
        mesh=mesh,
        in_specs=placed,
        out_specs=P(("sta", "grp"), None, None),
        check_vma=False,
    )
```

```python
import functools
import math

import jax
import jax.numpy as jnp
import ml_dtypes
import numpy as np
from jax import lax
from jax.experimental import pallas as pl
from jax.experimental.pallas import tpu as pltpu
from jax.sharding import PartitionSpec as P

LAGS = 1024
two_pi = 2.0 * math.pi
MESH = pl.DeviceIdType.MESH


def lag_table(num_bins, chunk):
    period = 2 * num_bins
    shift = np.arange(LAGS) - LAGS // 2
    angles = np.mod(np.arange(num_bins)[:, None] * shift[None, :], period).astype(np.float32) * np.float32(two_pi / period)
    both = np.stack([np.cos(angles), -np.sin(angles)]).reshape(2, num_bins // chunk, chunk, LAGS)
    return both.transpose(1, 0, 2, 3).reshape(2 * num_bins, LAGS).astype(ml_dtypes.bfloat16)


def kernel(
    n, groups, hours, pairs, chunk, chunks, helped, ahead, slack, scale,
    spec_ref, pick_ref, table_ref,
    out_ref,
    gathered, picks, table, src, rcv, cross, acc, partial, paired, mid, landed, final,
    handed,
    send_sem, recv_sem, pick_send, pick_recv, give_send, give_recv, pair_send, pair_recv, part_send, part_recv, fin_send, fin_recv,
    hand_send, hand_recv, table_sem,
):
    z = lax.axis_index("sta")
    g = lax.axis_index("grp")
    h = lax.axis_index("hr")
    plane = groups * hours
    me = g * hours + h
    block = spec_ref.shape[0]
    pick_rows = pick_ref.shape[0]
    rows = 9 * pairs
    part = LAGS // hours
    edge = (z == 0) | (z == n - 1)
    helper = (z == 1) | (z == n - 2)
    partner = jnp.where(z == 0, 1, jnp.where(z == 1, 0, jnp.where(z == n - 1, n - 2, n - 1)))

    for c in range(chunks):
        gathered[c, pl.ds(pl.multiple_of(z * block, 16), block), :] = spec_ref[:, c * chunk:(c + 1) * chunk]

    def table_copy(c):
        return pltpu.make_async_copy(
            table_ref.at[pl.ds(pl.multiple_of((g * chunks + c) * (2 * chunk), 16), 2 * chunk)],
            table.at[pl.ds(pl.multiple_of(c * (2 * chunk), 16), 2 * chunk)],
            table_sem.at[c],
        )

    barrier = pltpu.get_barrier_semaphore()

    @pl.loop(1, plane)
    def _(d):
        t = lax.rem(me + d, plane)
        pl.semaphore_signal(
            barrier, inc=1, device_id={"grp": t // hours, "hr": lax.rem(t, hours)}, device_id_type=MESH
        )

    @pl.when(z > 0)
    def _():
        pl.semaphore_signal(barrier, inc=1, device_id={"sta": z - 1}, device_id_type=MESH)

    @pl.when(z < n - 1)
    def _():
        pl.semaphore_signal(barrier, inc=1, device_id={"sta": z + 1}, device_id_type=MESH)

    expected = plane - 1 + (z > 0).astype(jnp.int32) + (z < n - 1).astype(jnp.int32)
    if helped:
        @pl.when(edge | helper)
        def _():
            @pl.loop(1, groups)
            def _(d):
                pl.semaphore_signal(
                    barrier, inc=1, device_id={"sta": partner, "grp": lax.rem(g + d, groups)}, device_id_type=MESH
                )

        expected = expected + (groups - 1) * (edge | helper).astype(jnp.int32)
    pl.semaphore_wait(barrier, expected)

    def line_copy(b, c, side):
        spot = gathered.at[c, pl.ds(pl.multiple_of(b * block, 16), block)]
        return pltpu.make_async_remote_copy(
            src_ref=spot,
            dst_ref=spot,
            send_sem=send_sem.at[side, b, c],
            recv_sem=recv_sem.at[b, c],
            device_id={"sta": z + 1 if side == 0 else z - 1},
            device_id_type=MESH,
        )

    def goes_right(c):
        return (z < n - 2) | ((z == n - 2) & (c >= helped))

    def goes_left(c):
        return (z > 1) | ((z == 1) & (c >= helped))

    def send_own(c):
        @pl.when(goes_right(c))
        def _():
            line_copy(z, c, 0).start()

        @pl.when(goes_left(c))
        def _():
            line_copy(z, c, 1).start()

    def pick_copy(d):
        return pltpu.make_async_remote_copy(
            src_ref=pick_ref,
            dst_ref=picks.at[0, pl.ds(pl.multiple_of(g * pick_rows, 16), pick_rows)],
            send_sem=pick_send.at[d],
            recv_sem=pick_recv.at[d],
            device_id={"grp": lax.rem(g + d, groups)},
            device_id_type=MESH,
        )

    def give_copy(d):
        return pltpu.make_async_remote_copy(
            src_ref=pick_ref,
            dst_ref=picks.at[1, pl.ds(pl.multiple_of(g * pick_rows, 16), pick_rows)],
            send_sem=give_send.at[d],
            recv_sem=give_recv.at[d],
            device_id={"sta": partner, "grp": lax.rem(g + d, groups)},
            device_id_type=MESH,
        )

    at_once = jnp.where(edge, chunks, min(ahead, chunks))

    @pl.loop(0, at_once)
    def _(c):
        send_own(c)

    @pl.loop(0, chunks)
    def _(c):
        table_copy(c).start()

    @pl.loop(1, groups)
    def _(d):
        pick_copy(d).start()

    if helped:
        @pl.when(edge)
        def _():
            @pl.loop(0, groups)
            def _(d):
                give_copy(d).start()

    picks[0, pl.ds(pl.multiple_of(g * pick_rows, 16), pick_rows), :] = pick_ref[...]
    acc[...] = jnp.zeros_like(acc)

    def arrive(k, c):
        wanted = (c >= helped) | jnp.logical_not(edge)

        @pl.when((z - k >= 0) & wanted)
        def _():
            line_copy(z - k, c, 0).wait_recv()

            @pl.when(goes_right(c))
            def _():
                line_copy(z - k, c, 0).start()

        @pl.when((z + k < n) & wanted)
        def _():
            line_copy(z + k, c, 1).wait_recv()

            @pl.when(goes_left(c))
            def _():
                line_copy(z + k, c, 1).start()

    def compute(w, c):
        origin = jnp.where(w == 0, z, partner)
        own = gathered[c, pl.ds(pl.multiple_of(origin * block, 16), block), :]
        src[...] = jnp.dot(
            picks[w, :, n * block:(n + 1) * block], own, preferred_element_type=jnp.float32
        )
        rcv[...] = jnp.dot(
            picks[w, :, 0:n * block], gathered[c], preferred_element_type=jnp.float32
        )

        @pl.loop(0, groups)
        def _(q):
            base = pl.multiple_of(q * pick_rows, 16)
            top = pl.multiple_of(q * rows, 16)
            for lane in range(0, chunk, 128):
                s = [src[pl.ds(base + pairs * k, pairs), lane:lane + 128] for k in range(6)]
                r = [rcv[pl.ds(base + pairs * k, pairs), lane:lane + 128] for k in range(6)]
                for a in range(3):
                    for b in range(3):
                        spot = pl.ds(top + (3 * a + b) * pairs, pairs)
                        cross[spot, lane:lane + 128] = (s[a] * r[b] + s[3 + a] * r[3 + b]).astype(jnp.bfloat16)
                        cross[spot, chunk + lane:chunk + lane + 128] = (
                            s[a] * r[3 + b] - s[3 + a] * r[b]
                        ).astype(jnp.bfloat16)

        acc[w] += jnp.dot(
            cross[...],
            table[pl.ds(pl.multiple_of(c * (2 * chunk), 16), 2 * chunk), :],
            preferred_element_type=jnp.float32,
        )

    quads = hours // 2
    q, odd = h // 2, lax.rem(h, 2)
    half = quads * part
    my_half = pl.ds(pl.multiple_of(odd * half, 128), half)
    other_half = pl.ds(pl.multiple_of((1 - odd) * half, 128), half)
    in_half = pl.ds(pl.multiple_of(q * part, 128), part)
    lag_start = odd * half + q * part
    lags = pl.ds(pl.multiple_of(lag_start, 128), part)
    own_rows = pl.ds(pl.multiple_of(g * rows, 16), rows)
    owners = groups * quads

    def pair_copy(w):
        return pltpu.make_async_remote_copy(
            src_ref=partial.at[w],
            dst_ref=paired.at[w],
            send_sem=pair_send.at[w],
            recv_sem=pair_recv.at[w],
            device_id={"hr": 2 * q + (1 - odd)},
            device_id_type=MESH,
        )

    def part_copy(w, d):
        t = lax.rem(g * quads + q + d, owners)
        tg, tq = t // quads, lax.rem(t, quads)
        return pltpu.make_async_remote_copy(
            src_ref=mid.at[
                w, pl.ds(pl.multiple_of(tg * rows, 16), rows), pl.ds(pl.multiple_of(tq * part, 128), part)
            ],
            dst_ref=landed.at[w, d],
            send_sem=part_send.at[w, d],
            recv_sem=part_recv.at[w, d],
            device_id={"grp": tg, "hr": 2 * tq + odd},
            device_id_type=MESH,
        )

    def pair_up(w):
        partial[w] = acc[w, :, other_half].astype(jnp.bfloat16)
        pair_copy(w).start()

    def scatter(w):
        pair_copy(w).wait_recv()
        mid[w] = (acc[w, :, my_half] + paired[w].astype(jnp.float32)).astype(jnp.bfloat16)

        @pl.loop(1, owners)
        def _(d):
            part_copy(w, d).start()

    def collect(w):
        final[...] = acc[w, own_rows, lags] + paired[w, own_rows, in_half].astype(jnp.float32)

        @pl.loop(1, owners)
        def _(d):
            part_copy(w, d).wait_recv()
            final[...] += landed[w, d].astype(jnp.float32)

    def hand_copy():
        return pltpu.make_async_remote_copy(
            src_ref=handed,
            dst_ref=landed.at[0, 0],
            send_sem=hand_send,
            recv_sem=hand_recv,
            device_id={"sta": partner},
            device_id_type=MESH,
        )

    lag_steps = slack * (jnp.maximum(z, n - 1 - z) - 1)

    @pl.loop(0, chunks + slack * max(n - 2, 0))
    def _(it):
        @pl.when((it + ahead < chunks) & jnp.logical_not(edge))
        def _():
            send_own(it + ahead)

        @pl.loop(1, n)
        def _(back):
            k = n - back
            c = it - slack * (k - 1)

            @pl.when((c >= 0) & (c < chunks))
            def _():
                arrive(k, c)

        @pl.when(it == lag_steps)
        def _():
            @pl.loop(1, groups)
            def _(d):
                pick_copy(d).wait()

            if helped:
                @pl.when(helper)
                def _():
                    @pl.loop(0, groups)
                    def _(d):
                        give_copy(d).wait_recv()

        c = it - lag_steps
        @pl.when((c >= 0) & (c < chunks))
        def _():
            table_copy(c).wait()

        turns = jnp.where(c >= helped, 1, jnp.where(edge, 0, jnp.where(helper, 2, 1)))

        @pl.loop(0, jnp.where((c >= 0) & (c < chunks), turns, 0))
        def _(w):
            compute(w, c)

        if helped:
            @pl.when(helper & (c == helped - 1))
            def _():
                pair_up(1)

            @pl.when(helper & (c == helped))
            def _():
                scatter(1)

    pair_up(0)
    if helped:
        @pl.when(helper)
        def _():
            collect(1)
            handed[...] = final[...].astype(jnp.bfloat16)
            hand_copy().start()

    scatter(0)
    collect(0)
    if helped:
        @pl.when(edge)
        def _():
            hand_copy().wait_recv()
            final[...] += landed[0, 0].astype(jnp.float32)

    lag = (lag_start + lax.broadcasted_iota(jnp.int32, (8, part), 1)).astype(jnp.float32)
    taper = (0.75 - 0.25 * jnp.cos(two_pi * (lag + 0.5) / LAGS)) * scale
    out_ref[:, lags] = (final[...] * taper[0:1, :]).astype(jnp.bfloat16)

    def fin_copy(d):
        return pltpu.make_async_remote_copy(
            src_ref=out_ref.at[:, lags],
            dst_ref=out_ref.at[:, lags],
            send_sem=fin_send.at[d],
            recv_sem=fin_recv.at[d],
            device_id={"hr": lax.rem(h + d, hours)},
            device_id_type=MESH,
        )

    @pl.loop(1, hours)
    def _(d):
        fin_copy(d).start()

    pair_copy(0).wait_send()

    @pl.loop(1, owners)
    def _(d):
        part_copy(0, d).wait_send()

    if helped:
        @pl.when(helper)
        def _():
            hand_copy().wait_send()
            pair_copy(1).wait_send()

            @pl.loop(1, owners)
            def _(d):
                part_copy(1, d).wait_send()

        @pl.when(edge)
        def _():
            @pl.loop(0, groups)
            def _(d):
                give_copy(d).wait_send()

    @pl.loop(0, n - 1)
    def _(k):
        @pl.loop(0, chunks)
        def _(c):
            @pl.when((z - k >= 0) & goes_right(c))
            def _():
                line_copy(z - k, c, 0).wait_send()

            @pl.when((z + k < n) & goes_left(c))
            def _():
                line_copy(z + k, c, 1).wait_send()

    @pl.loop(1, hours)
    def _(d):
        fin_copy(d).wait()


def body(n, groups, hours, spectra, pair_source, pair_owner, pair_row):
    _, sta_dev, comps, num_bins = spectra.shape
    pairs = pair_source.shape[0]
    bins = num_bins // groups
    chunk = min(512, bins)
    chunks = bins // chunk
    helped = 5 * chunks // 16 if n >= 4 else 0
    held = 2 if helped else 1
    block = comps * sta_dev
    pick_rows = comps * pairs
    width = -(-((n + 1) * block) // 128) * 128

    start = lax.axis_index("grp") * bins
    mine = lax.dynamic_slice_in_dim(spectra[0], start, bins, 2)
    spec = jnp.transpose(mine, (1, 0, 2)).reshape(block, bins)

    comp_at = (jnp.arange(comps, dtype=jnp.int32) * sta_dev)[:, None]
    wanted = (comp_at + (pair_owner[:, 0] * block + pair_row)[None, :]).reshape(pick_rows, 1)
    origin = (comp_at + (n * block + pair_source)[None, :]).reshape(pick_rows, 1)
    column = jnp.arange(width, dtype=jnp.int32)[None, :]
    pick = ((wanted == column) | (origin == column)).astype(jnp.bfloat16)

    scale = 1.0 / (hours * spectra.shape[0] * math.sqrt(num_bins))
    rows = 9 * pairs
    vmem = pl.BlockSpec(memory_space=pltpu.VMEM)
    out = pl.pallas_call(
        functools.partial(kernel, n, groups, hours, pairs, chunk, chunks, helped, 3, 2, scale),
        out_shape=jax.ShapeDtypeStruct((rows, LAGS), jnp.bfloat16),
        in_specs=[vmem, vmem, pl.BlockSpec(memory_space=pltpu.HBM)],
        out_specs=vmem,
        scratch_shapes=[
            pltpu.VMEM((chunks, n * block, chunk), jnp.bfloat16),
            pltpu.VMEM((held, groups * pick_rows, width), jnp.bfloat16),
            pltpu.VMEM((2 * bins, LAGS), jnp.bfloat16),
            pltpu.VMEM((groups * pick_rows, chunk), jnp.float32),
            pltpu.VMEM((groups * pick_rows, chunk), jnp.float32),
            pltpu.VMEM((groups * rows, 2 * chunk), jnp.bfloat16),
            pltpu.VMEM((held, groups * rows, LAGS), jnp.float32),
            pltpu.VMEM((held, groups * rows, LAGS // 2), jnp.bfloat16),
            pltpu.VMEM((held, groups * rows, LAGS // 2), jnp.bfloat16),
            pltpu.VMEM((held, groups * rows, LAGS // 2), jnp.bfloat16),
            pltpu.VMEM((held, groups * hours // 2, rows, LAGS // hours), jnp.bfloat16),
            pltpu.VMEM((rows, LAGS // hours), jnp.float32),
            pltpu.VMEM((rows, LAGS // hours), jnp.bfloat16),
            pltpu.SemaphoreType.DMA((2, n, chunks)),
            pltpu.SemaphoreType.DMA((n, chunks)),
            pltpu.SemaphoreType.DMA((groups,)),
            pltpu.SemaphoreType.DMA((groups,)),
            pltpu.SemaphoreType.DMA((groups,)),
            pltpu.SemaphoreType.DMA((groups,)),
            pltpu.SemaphoreType.DMA((held,)),
            pltpu.SemaphoreType.DMA((held,)),
            pltpu.SemaphoreType.DMA((held, groups * hours // 2)),
            pltpu.SemaphoreType.DMA((held, groups * hours // 2)),
            pltpu.SemaphoreType.DMA((hours,)),
            pltpu.SemaphoreType.DMA((hours,)),
            pltpu.SemaphoreType.DMA,
            pltpu.SemaphoreType.DMA,
            pltpu.SemaphoreType.DMA((chunks,)),
        ],
        compiler_params=pltpu.CompilerParams(
            collective_id=0, has_side_effects=True, vmem_limit_bytes=48 * 1024 * 1024
        ),
        cost_estimate=pl.CostEstimate(
            flops=4 * groups * rows * bins * LAGS, bytes_accessed=4 * block * bins, transcendentals=0
        ),
    )(spec, pick, jnp.asarray(lag_table(num_bins, chunk)))
    return jnp.transpose(out.reshape(9, pairs, LAGS), (1, 0, 2)).astype(jnp.float32)


def solution(mesh):
    placed = (
        P("hr", "sta", None, None),
        P(("sta", "grp")),
        P(("sta", "grp"), None),
        P(("sta", "grp")),
    )
    sizes = (mesh.shape["sta"], mesh.shape["grp"], mesh.shape["hr"])
    return jax.shard_map(
        functools.partial(body, *sizes),
        mesh=mesh,
        in_specs=placed,
        out_specs=P(("sta", "grp"), None, None),
        check_vma=False,
    )
```

```python
import functools
import math

import jax
import jax.numpy as jnp
import ml_dtypes
import numpy as np
from jax import lax
from jax.experimental import pallas as pl
from jax.experimental.pallas import tpu as pltpu
from jax.sharding import PartitionSpec as P

LAGS = 1024
two_pi = 2.0 * math.pi
MESH = pl.DeviceIdType.MESH


def lag_table(num_bins, chunk):
    period = 2 * num_bins
    shift = np.arange(LAGS) - LAGS // 2
    angles = np.mod(np.arange(num_bins)[:, None] * shift[None, :], period).astype(np.float32) * np.float32(two_pi / period)
    both = np.stack([np.cos(angles), -np.sin(angles)]).reshape(2, num_bins // chunk, chunk, LAGS)
    return both.transpose(1, 0, 2, 3).reshape(2 * num_bins, LAGS).astype(ml_dtypes.bfloat16)


def kernel(
    n, groups, hours, pairs, chunk, chunks, helped, ahead, slack, scale,
    spec_ref, pick_ref, table_ref,
    out_ref,
    gathered, picks, table, src, rcv, cross, acc, partial, paired, mid, landed, final,
    handed,
    send_sem, recv_sem, pick_send, pick_recv, give_send, give_recv, pair_send, pair_recv, part_send, part_recv, fin_send, fin_recv,
    hand_send, hand_recv, table_sem,
):
    z = lax.axis_index("sta")
    g = lax.axis_index("grp")
    h = lax.axis_index("hr")
    plane = groups * hours
    me = g * hours + h
    block = spec_ref.shape[0]
    pick_rows = pick_ref.shape[0]
    rows = 9 * pairs
    part = LAGS // hours
    edge = (z == 0) | (z == n - 1)
    helper = (z == 1) | (z == n - 2)
    partner = jnp.where(z == 0, 1, jnp.where(z == 1, 0, jnp.where(z == n - 1, n - 2, n - 1)))

    for c in range(chunks):
        gathered[c, pl.ds(pl.multiple_of(z * block, 16), block), :] = spec_ref[:, c * chunk:(c + 1) * chunk]

    def table_copy(c):
        return pltpu.make_async_copy(
            table_ref.at[pl.ds(pl.multiple_of((g * chunks + c) * (2 * chunk), 16), 2 * chunk)],
            table.at[pl.ds(pl.multiple_of(c * (2 * chunk), 16), 2 * chunk)],
            table_sem.at[c],
        )

    barrier = pltpu.get_barrier_semaphore()

    @pl.loop(1, plane)
    def _(d):
        t = lax.rem(me + d, plane)
        pl.semaphore_signal(
            barrier, inc=1, device_id={"grp": t // hours, "hr": lax.rem(t, hours)}, device_id_type=MESH
        )

    @pl.when(z > 0)
    def _():
        pl.semaphore_signal(barrier, inc=1, device_id={"sta": z - 1}, device_id_type=MESH)

    @pl.when(z < n - 1)
    def _():
        pl.semaphore_signal(barrier, inc=1, device_id={"sta": z + 1}, device_id_type=MESH)

    expected = plane - 1 + (z > 0).astype(jnp.int32) + (z < n - 1).astype(jnp.int32)
    if helped:
        @pl.when(edge | helper)
        def _():
            @pl.loop(1, groups)
            def _(d):
                pl.semaphore_signal(
                    barrier, inc=1, device_id={"sta": partner, "grp": lax.rem(g + d, groups)}, device_id_type=MESH
                )

        expected = expected + (groups - 1) * (edge | helper).astype(jnp.int32)
    pl.semaphore_wait(barrier, expected)

    def line_copy(b, c, side):
        spot = gathered.at[c, pl.ds(pl.multiple_of(b * block, 16), block)]
        return pltpu.make_async_remote_copy(
            src_ref=spot,
            dst_ref=spot,
            send_sem=send_sem.at[side, b, c],
            recv_sem=recv_sem.at[b, c],
            device_id={"sta": z + 1 if side == 0 else z - 1},
            device_id_type=MESH,
        )

    def goes_right(c):
        return (z < n - 2) | ((z == n - 2) & (c >= helped))

    def goes_left(c):
        return (z > 1) | ((z == 1) & (c >= helped))

    def send_own(c):
        @pl.when(goes_right(c))
        def _():
            line_copy(z, c, 0).start()

        @pl.when(goes_left(c))
        def _():
            line_copy(z, c, 1).start()

    def pick_copy(d):
        return pltpu.make_async_remote_copy(
            src_ref=pick_ref,
            dst_ref=picks.at[0, pl.ds(pl.multiple_of(g * pick_rows, 16), pick_rows)],
            send_sem=pick_send.at[d],
            recv_sem=pick_recv.at[d],
            device_id={"grp": lax.rem(g + d, groups)},
            device_id_type=MESH,
        )

    def give_copy(d):
        return pltpu.make_async_remote_copy(
            src_ref=pick_ref,
            dst_ref=picks.at[1, pl.ds(pl.multiple_of(g * pick_rows, 16), pick_rows)],
            send_sem=give_send.at[d],
            recv_sem=give_recv.at[d],
            device_id={"sta": partner, "grp": lax.rem(g + d, groups)},
            device_id_type=MESH,
        )

    @pl.loop(0, min(ahead, chunks))
    def _(c):
        send_own(c)

    @pl.loop(0, chunks)
    def _(c):
        table_copy(c).start()

    @pl.loop(1, groups)
    def _(d):
        pick_copy(d).start()

    if helped:
        @pl.when(edge)
        def _():
            @pl.loop(0, groups)
            def _(d):
                give_copy(d).start()

    picks[0, pl.ds(pl.multiple_of(g * pick_rows, 16), pick_rows), :] = pick_ref[...]
    acc[...] = jnp.zeros_like(acc)

    def arrive(k, c):
        wanted = (c >= helped) | jnp.logical_not(edge)

        @pl.when((z - k >= 0) & wanted)
        def _():
            line_copy(z - k, c, 0).wait_recv()

            @pl.when(goes_right(c))
            def _():
                line_copy(z - k, c, 0).start()

        @pl.when((z + k < n) & wanted)
        def _():
            line_copy(z + k, c, 1).wait_recv()

            @pl.when(goes_left(c))
            def _():
                line_copy(z + k, c, 1).start()

    def compute(w, c):
        origin = jnp.where(w == 0, z, partner)
        own = gathered[c, pl.ds(pl.multiple_of(origin * block, 16), block), :]
        src[...] = jnp.dot(
            picks[w, :, n * block:(n + 1) * block], own, preferred_element_type=jnp.float32
        )
        rcv[...] = jnp.dot(
            picks[w, :, 0:n * block], gathered[c], preferred_element_type=jnp.float32
        )

        @pl.loop(0, groups)
        def _(q):
            base = pl.multiple_of(q * pick_rows, 16)
            top = pl.multiple_of(q * rows, 16)
            for lane in range(0, chunk, 128):
                s = [src[pl.ds(base + pairs * k, pairs), lane:lane + 128] for k in range(6)]
                r = [rcv[pl.ds(base + pairs * k, pairs), lane:lane + 128] for k in range(6)]
                for a in range(3):
                    for b in range(3):
                        spot = pl.ds(top + (3 * a + b) * pairs, pairs)
                        cross[spot, lane:lane + 128] = (s[a] * r[b] + s[3 + a] * r[3 + b]).astype(jnp.bfloat16)
                        cross[spot, chunk + lane:chunk + lane + 128] = (
                            s[a] * r[3 + b] - s[3 + a] * r[b]
                        ).astype(jnp.bfloat16)

        acc[w] += jnp.dot(
            cross[...],
            table[pl.ds(pl.multiple_of(c * (2 * chunk), 16), 2 * chunk), :],
            preferred_element_type=jnp.float32,
        )

    quads = hours // 2
    q, odd = h // 2, lax.rem(h, 2)
    half = quads * part
    my_half = pl.ds(pl.multiple_of(odd * half, 128), half)
    other_half = pl.ds(pl.multiple_of((1 - odd) * half, 128), half)
    in_half = pl.ds(pl.multiple_of(q * part, 128), part)
    lag_start = odd * half + q * part
    lags = pl.ds(pl.multiple_of(lag_start, 128), part)
    own_rows = pl.ds(pl.multiple_of(g * rows, 16), rows)
    owners = groups * quads

    def pair_copy(w):
        return pltpu.make_async_remote_copy(
            src_ref=partial.at[w],
            dst_ref=paired.at[w],
            send_sem=pair_send.at[w],
            recv_sem=pair_recv.at[w],
            device_id={"hr": 2 * q + (1 - odd)},
            device_id_type=MESH,
        )

    def part_copy(w, d):
        t = lax.rem(g * quads + q + d, owners)
        tg, tq = t // quads, lax.rem(t, quads)
        return pltpu.make_async_remote_copy(
            src_ref=mid.at[
                w, pl.ds(pl.multiple_of(tg * rows, 16), rows), pl.ds(pl.multiple_of(tq * part, 128), part)
            ],
            dst_ref=landed.at[w, d],
            send_sem=part_send.at[w, d],
            recv_sem=part_recv.at[w, d],
            device_id={"grp": tg, "hr": 2 * tq + odd},
            device_id_type=MESH,
        )

    def pair_up(w):
        partial[w] = acc[w, :, other_half].astype(jnp.bfloat16)
        pair_copy(w).start()

    def scatter(w):
        pair_copy(w).wait_recv()
        mid[w] = (acc[w, :, my_half] + paired[w].astype(jnp.float32)).astype(jnp.bfloat16)

        @pl.loop(1, owners)
        def _(d):
            part_copy(w, d).start()

    def collect(w):
        final[...] = acc[w, own_rows, lags] + paired[w, own_rows, in_half].astype(jnp.float32)

        @pl.loop(1, owners)
        def _(d):
            part_copy(w, d).wait_recv()
            final[...] += landed[w, d].astype(jnp.float32)

    def hand_copy():
        return pltpu.make_async_remote_copy(
            src_ref=handed,
            dst_ref=landed.at[0, 0],
            send_sem=hand_send,
            recv_sem=hand_recv,
            device_id={"sta": partner},
            device_id_type=MESH,
        )

    lag_steps = slack * (jnp.maximum(z, n - 1 - z) - 1)

    @pl.loop(0, chunks + slack * max(n - 2, 0))
    def _(it):
        @pl.when(it + ahead < chunks)
        def _():
            send_own(it + ahead)

        @pl.loop(1, n)
        def _(k):
            c = it - slack * (k - 1)

            @pl.when((c >= 0) & (c < chunks))
            def _():
                arrive(k, c)

        @pl.when(it == lag_steps)
        def _():
            @pl.loop(1, groups)
            def _(d):
                pick_copy(d).wait()

            if helped:
                @pl.when(helper)
                def _():
                    @pl.loop(0, groups)
                    def _(d):
                        give_copy(d).wait_recv()

        c = it - lag_steps
        @pl.when((c >= 0) & (c < chunks))
        def _():
            table_copy(c).wait()

        turns = jnp.where(c >= helped, 1, jnp.where(edge, 0, jnp.where(helper, 2, 1)))

        @pl.loop(0, jnp.where((c >= 0) & (c < chunks), turns, 0))
        def _(w):
            compute(w, c)

        if helped:
            @pl.when(helper & (c == helped - 1))
            def _():
                pair_up(1)

            @pl.when(helper & (c == helped))
            def _():
                scatter(1)

    pair_up(0)
    if helped:
        @pl.when(helper)
        def _():
            collect(1)
            handed[...] = final[...].astype(jnp.bfloat16)
            hand_copy().start()

    scatter(0)
    collect(0)
    if helped:
        @pl.when(edge)
        def _():
            hand_copy().wait_recv()
            final[...] += landed[0, 0].astype(jnp.float32)

    lag = (lag_start + lax.broadcasted_iota(jnp.int32, (8, part), 1)).astype(jnp.float32)
    taper = (0.75 - 0.25 * jnp.cos(two_pi * (lag + 0.5) / LAGS)) * scale
    out_ref[:, lags] = (final[...] * taper[0:1, :]).astype(jnp.bfloat16)

    def fin_copy(d):
        return pltpu.make_async_remote_copy(
            src_ref=out_ref.at[:, lags],
            dst_ref=out_ref.at[:, lags],
            send_sem=fin_send.at[d],
            recv_sem=fin_recv.at[d],
            device_id={"hr": lax.rem(h + d, hours)},
            device_id_type=MESH,
        )

    @pl.loop(1, hours)
    def _(d):
        fin_copy(d).start()

    pair_copy(0).wait_send()

    @pl.loop(1, owners)
    def _(d):
        part_copy(0, d).wait_send()

    if helped:
        @pl.when(helper)
        def _():
            hand_copy().wait_send()
            pair_copy(1).wait_send()

            @pl.loop(1, owners)
            def _(d):
                part_copy(1, d).wait_send()

        @pl.when(edge)
        def _():
            @pl.loop(0, groups)
            def _(d):
                give_copy(d).wait_send()

    @pl.loop(0, n - 1)
    def _(k):
        @pl.loop(0, chunks)
        def _(c):
            @pl.when((z - k >= 0) & goes_right(c))
            def _():
                line_copy(z - k, c, 0).wait_send()

            @pl.when((z + k < n) & goes_left(c))
            def _():
                line_copy(z + k, c, 1).wait_send()

    @pl.loop(1, hours)
    def _(d):
        fin_copy(d).wait()


def body(n, groups, hours, spectra, pair_source, pair_owner, pair_row):
    _, sta_dev, comps, num_bins = spectra.shape
    pairs = pair_source.shape[0]
    bins = num_bins // groups
    chunk = min(512, bins)
    chunks = bins // chunk
    helped = chunks // 2 if n >= 4 else 0
    held = 2 if helped else 1
    block = comps * sta_dev
    pick_rows = comps * pairs
    width = -(-((n + 1) * block) // 128) * 128

    start = lax.axis_index("grp") * bins
    mine = lax.dynamic_slice_in_dim(spectra[0], start, bins, 2)
    spec = jnp.transpose(mine, (1, 0, 2)).reshape(block, bins)

    comp_at = (jnp.arange(comps, dtype=jnp.int32) * sta_dev)[:, None]
    wanted = (comp_at + (pair_owner[:, 0] * block + pair_row)[None, :]).reshape(pick_rows, 1)
    origin = (comp_at + (n * block + pair_source)[None, :]).reshape(pick_rows, 1)
    column = jnp.arange(width, dtype=jnp.int32)[None, :]
    pick = ((wanted == column) | (origin == column)).astype(jnp.bfloat16)

    scale = 1.0 / (hours * spectra.shape[0] * math.sqrt(num_bins))
    rows = 9 * pairs
    vmem = pl.BlockSpec(memory_space=pltpu.VMEM)
    out = pl.pallas_call(
        functools.partial(kernel, n, groups, hours, pairs, chunk, chunks, helped, 3, 2, scale),
        out_shape=jax.ShapeDtypeStruct((rows, LAGS), jnp.bfloat16),
        in_specs=[vmem, vmem, pl.BlockSpec(memory_space=pltpu.HBM)],
        out_specs=vmem,
        scratch_shapes=[
            pltpu.VMEM((chunks, n * block, chunk), jnp.bfloat16),
            pltpu.VMEM((held, groups * pick_rows, width), jnp.bfloat16),
            pltpu.VMEM((2 * bins, LAGS), jnp.bfloat16),
            pltpu.VMEM((groups * pick_rows, chunk), jnp.float32),
            pltpu.VMEM((groups * pick_rows, chunk), jnp.float32),
            pltpu.VMEM((groups * rows, 2 * chunk), jnp.bfloat16),
            pltpu.VMEM((held, groups * rows, LAGS), jnp.float32),
            pltpu.VMEM((held, groups * rows, LAGS // 2), jnp.bfloat16),
            pltpu.VMEM((held, groups * rows, LAGS // 2), jnp.bfloat16),
            pltpu.VMEM((held, groups * rows, LAGS // 2), jnp.bfloat16),
            pltpu.VMEM((held, groups * hours // 2, rows, LAGS // hours), jnp.bfloat16),
            pltpu.VMEM((rows, LAGS // hours), jnp.float32),
            pltpu.VMEM((rows, LAGS // hours), jnp.bfloat16),
            pltpu.SemaphoreType.DMA((2, n, chunks)),
            pltpu.SemaphoreType.DMA((n, chunks)),
            pltpu.SemaphoreType.DMA((groups,)),
            pltpu.SemaphoreType.DMA((groups,)),
            pltpu.SemaphoreType.DMA((groups,)),
            pltpu.SemaphoreType.DMA((groups,)),
            pltpu.SemaphoreType.DMA((held,)),
            pltpu.SemaphoreType.DMA((held,)),
            pltpu.SemaphoreType.DMA((held, groups * hours // 2)),
            pltpu.SemaphoreType.DMA((held, groups * hours // 2)),
            pltpu.SemaphoreType.DMA((hours,)),
            pltpu.SemaphoreType.DMA((hours,)),
            pltpu.SemaphoreType.DMA,
            pltpu.SemaphoreType.DMA,
            pltpu.SemaphoreType.DMA((chunks,)),
        ],
        compiler_params=pltpu.CompilerParams(
            collective_id=0, has_side_effects=True, vmem_limit_bytes=48 * 1024 * 1024
        ),
        cost_estimate=pl.CostEstimate(
            flops=4 * groups * rows * bins * LAGS, bytes_accessed=4 * block * bins, transcendentals=0
        ),
    )(spec, pick, jnp.asarray(lag_table(num_bins, chunk)))
    return jnp.transpose(out.reshape(9, pairs, LAGS), (1, 0, 2)).astype(jnp.float32)


def solution(mesh):
    placed = (
        P("hr", "sta", None, None),
        P(("sta", "grp")),
        P(("sta", "grp"), None),
        P(("sta", "grp")),
    )
    sizes = (mesh.shape["sta"], mesh.shape["grp"], mesh.shape["hr"])
    return jax.shard_map(
        functools.partial(body, *sizes),
        mesh=mesh,
        in_specs=placed,
        out_specs=P(("sta", "grp"), None, None),
        check_vma=False,
    )
```
